256 devices in a mesh: sec: 4 (over x), ep: 64 (over y, z, core).
Axes of the slice: x: 4, y: 4, z: 8, core: 2. Of those that a mesh axis runs over, the one named last changes fastest.
Arguments:
- residual_in: bfloat16 [128, 6144], P('ep', 'sec'), may hold values from -6 to 6
- queries: bfloat16 [128, 8192], P('sec', 'ep'), may hold values from -6 to 6
- keys_new: bfloat16 [128, 8192], P('sec', 'ep'), may hold values from -6 to 6
- values_new: bfloat16 [128, 8192], P('sec', 'ep'), may hold values from -6 to 6
- cached_state: float32 [128, 64, 128, 128], P('sec', 'ep'), may hold values from -6 to 6
- incoming_state: float32 [16, 64, 128, 128], P('sec', None, 'ep'), may hold values from -6 to 6
- admit_slot: int32 [16], P('sec'), may hold values from 0 to 127, as said below
- occupancy: int32 [128], P('sec'), may hold values 0 or 1
- decay_rate: float32 [64], P('ep'), may hold values from 0.05 to 3
- out_proj: bfloat16 [8192, 6144], P('ep', 'sec'), may hold values from -0.0625 to 0.0625
- norm_gain: float32 [6144], replicated, may hold values from 0.1 to 1.9
- routes: int32 [128, 2], replicated, may hold values from 0 to 15, all different within a row; in each aligned block of 128 rows (0 to 127, 128 to 255, ...) at most 32 rows name the same one
- route_weight: float32 [128, 2], replicated, may hold values from 0.5 to 1.5
- gate_proj: bfloat16 [64, 6144, 1152], P('ep', None, 'sec'), may hold values from -0.078125 to 0.078125
- up_proj: bfloat16 [64, 6144, 1152], P('ep', None, 'sec'), may hold values from -0.078125 to 0.078125
- down_proj: bfloat16 [64, 1152, 6144], P('ep', 'sec'), may hold values from -0.09375 to 0.09375
Outputs:
- block_out: bfloat16 [128, 6144], P('ep', 'sec')
The draws below stay inside these ranges and needn't reach their ends.
Inputs may be any that keep to these rules, and one draw needn't show every extreme that they name: `admit_slot`: requests a with a // 4 = s take distinct slots among s * 32 to (s + 1) * 32 - 1. `routes`: A row's two experts differ; at most 32 rows name any one expert, a bound that some block reaches.
All inputs are finite; a program needn't handle non-finite values. No bound on the sum of `occupancy` on one device may be relied on, other than what follows from the above.
Results may differ from the reference program's by a relative error of at most 0.017.
Values may be sent and summed in bfloat16 or wider, within the bound.
A program may use at most 128 MiB of HBM per device.

```python
import math
import jax
import jax.numpy as jnp
import numpy as np
from jax import lax

D = 6144
HEADS = 64
HD = 128
EXPERTS = 16
FF = 4608
TOP = 2
ADMIT = 4
ROWS = 128
SLOTS_SEC = 32
NEW = 16
CAP = 32
PIECES = 64
FFP = 1152


def draw_admit_slot(key, part):
    key = jax.random.fold_in(key, 11)
    blocks = ROWS // SLOTS_SEC
    block_keys = jax.random.split(key, blocks)

    def one_block(block_key, block_index):
        shuffled = jax.random.permutation(block_key, SLOTS_SEC)
        return shuffled[:ADMIT] + block_index * SLOTS_SEC
    return jax.vmap(one_block)(block_keys, jnp.arange(blocks)).reshape(-1).astype(jnp.int32)


def set_ends(array, stream_key, low, largest):
    extent = array.shape
    place = [jax.random.randint(jax.random.fold_in(stream_key, axis), (), 0, extent[axis]) for axis in range(len(extent))]
    array = array.at[tuple(place)].set(low)
    longest = extent.index(max(extent))
    place[longest] = (place[longest] + 1) % extent[longest]
    return array.at[tuple(place)].set(largest)


def block_levels(key, extent, cuts, smallest, largest):
    def one(dim, parts):
        draws = jax.random.uniform(jax.random.fold_in(jax.random.fold_in(key, 6), dim), (parts,), jnp.float32, smallest / len(cuts), largest / len(cuts))
        return jnp.repeat(jnp.exp(draws), extent[dim] // parts).reshape((-1,) + (1,) * (len(extent) - dim - 1))

    loudness = one(*cuts[0])
    for cut in cuts[1:]:
        loudness = loudness * one(*cut)
    return loudness


def deal_out(own_key, own, number, rows, count, top, bound, slope):
    sequence = jax.random.permutation(own_key, count)
    heavy_load, common = portions_of(count, rows * top, bound, slope, True), portions_of(count, rows * top, bound, slope, False)
    places = jnp.arange(count)

    def named(sizes, offset_by):
        used = int((sizes > 0).sum())
        fixed = max(1, used // 4)
        moved = fixed + (places - fixed + offset_by * (used - fixed)) % max(1, count - fixed)
        return jnp.zeros((count,), jnp.int32).at[sequence[jnp.where(places < fixed, places, moved)]].set(jnp.asarray(sizes, jnp.int32))

    sizes = jnp.where(number % 4 == 0, named(heavy_load, number // 4), named(common, number - number // 4 - 1))
    mixed = jax.random.permutation(jax.random.fold_in(own, 3), count)
    giver, sink = mixed[0:count // 2 * 2:2], mixed[1:count // 2 * 2:2]
    room = jnp.minimum(sizes[giver] - 1, bound - sizes[sink]) // 2
    room = jnp.where((giver == sequence[0]) | (sink == sequence[0]) | (sizes[sink] == 0), 0, jnp.maximum(room, 0))
    moved = jax.random.randint(jax.random.fold_in(own, 4), (count // 2,), 0, 1 << 20) % (room + 1)
    sizes = sizes.at[giver].add(-moved).at[sink].add(moved)
    labels = jnp.searchsorted(jnp.cumsum(sizes), jnp.arange(rows * top), side="right").astype(jnp.int32)
    listing = labels.reshape(top, rows).T
    listing = listing[jax.random.permutation(jax.random.fold_in(own, 1), rows)]
    offset_by = jax.random.randint(jax.random.fold_in(own, 2), (rows, 1), 0, top)
    return jnp.take_along_axis(listing, (jnp.arange(top)[None, :] + offset_by) % top, axis=1)


def portions_of(count, total, limit, skew, full):
    weights = [(1 << 20) // math.isqrt(grade ** skew) + 1 for grade in range(1, count + 1)]
    largest = limit if full else min(limit, max(-(-total // count), total * weights[0] // sum(weights)))
    least = 1 if total - largest >= count - 1 else 0
    given, rest = [largest] + [least] * (count - 1), total - largest - least * (count - 1)
    while rest > 0:
        candidates = [i for i in range(1, count) if given[i] < largest] or [i for i in range(1, count) if given[i] < limit]
        whole, remaining = sum([weights[i] for i in candidates]), rest
        for i in candidates:
            more = min(limit - given[i], max(1, remaining * weights[i] // whole), rest)
            given[i] = given[i] + more
            rest = rest - more
    return np.array(given)


def bell_draw(rng, extent, deviation, limit, cuts=(), held_as=jnp.bfloat16):
    level = block_levels(rng, extent, cuts, -0.22, 0.18) if cuts else 1.0
    result = jax.random.normal(rng, extent, jnp.float32) * deviation * level
    return jnp.minimum(jnp.maximum(result, -limit), limit).astype(held_as)


def setup_inputs(seed: int = 0) -> dict:
    seeds = jax.random.split(jax.random.key(seed), 17)
    residual_in = bell_draw(seeds[0], (ROWS, D), 1.0, 6.0, ((0, 64), (1, 4)))
    queries = bell_draw(seeds[1], (ROWS, HEADS * HD), 1.0, 6.0, ((0, 4), (1, 64)))
    keys_new = bell_draw(seeds[2], (ROWS, HEADS * HD), 1.0, 6.0, ((0, 4), (1, 64)))
    values_new = bell_draw(seeds[3], (ROWS, HEADS * HD), 1.0, 6.0, ((0, 4), (1, 64)))
    cached_state = bell_draw(seeds[4], (ROWS, HEADS, HD, HD), 1.0, 6.0, ((0, 4), (1, 64)), jnp.float32)
    incoming_state = bell_draw(seeds[5], (NEW, HEADS, HD, HD), 1.0, 6.0, ((0, 4), (2, 64)), jnp.float32)
    admit_slot = draw_admit_slot(jax.random.fold_in(seeds[16], 71), 0)
    occupancy = set_ends((jax.random.randint(seeds[7], (ROWS,), 0, 4) < 3).astype(jnp.int32), jax.random.fold_in(seeds[7], 1), 0, 1)
    decay_rate = jnp.clip(jnp.exp(math.log(3.0) - 4.0943445 * jax.random.uniform(seeds[8], (HEADS,), jnp.float32) ** block_levels(seeds[8], (HEADS,), ((0, 64),), -0.2, 0.2)), 0.05, 3.0)
    out_proj = bell_draw(seeds[9], (HEADS * HD, D), (HEADS * HD) ** -0.5, 0.0625, ((0, 64), (1, 4)))
    norm_gain = jnp.clip(1.0 + 0.18 * jax.random.normal(seeds[10], (D,), jnp.float32), 0.1, 1.9)
    routes_keys = jax.random.split(jax.random.fold_in(seeds[11], 1), ROWS // ROWS)
    routes_turns = jax.random.permutation(jax.random.fold_in(seeds[11], 3), ROWS // ROWS)
    routes = jax.vmap(lambda own, number: deal_out(jax.random.fold_in(seeds[11], 2), own, number, ROWS, EXPERTS, TOP, CAP, 2))(routes_keys, routes_turns).reshape((ROWS, TOP))
    route_weight = jnp.clip(jax.random.uniform(seeds[12], (ROWS, TOP), jnp.float32, 0.5, 1.5), 0.5, 1.5)
    gate_proj = bell_draw(seeds[13], (PIECES, D, FFP), D ** -0.5, 0.078125, ((0, 64), (2, 4)))
    up_proj = bell_draw(seeds[14], (PIECES, D, FFP), D ** -0.5, 0.078125, ((0, 64), (2, 4)))
    down_proj = bell_draw(seeds[15], (PIECES, FFP, D), FF ** -0.5, 0.09375, ((0, 64), (1, 4)))
    return {"residual_in": residual_in, "queries": queries, "keys_new": keys_new, "values_new": values_new, "cached_state": cached_state, "incoming_state": incoming_state, "admit_slot": admit_slot, "occupancy": occupancy, "decay_rate": decay_rate, "out_proj": out_proj, "norm_gain": norm_gain, "routes": routes, "route_weight": route_weight, "gate_proj": gate_proj, "up_proj": up_proj, "down_proj": down_proj}


epsilon = 1e-06
exact_mode = lax.Precision.HIGHEST

def reference(residual_in, queries, keys_new, values_new, cached_state, incoming_state, admit_slot, occupancy, decay_rate, out_proj, norm_gain, routes, route_weight, gate_proj, up_proj, down_proj):
    query_rows = queries.astype(jnp.float32).reshape(ROWS, HEADS, HD)
    key_rows = keys_new.astype(jnp.float32).reshape(ROWS, HEADS, HD)
    value_rows = values_new.astype(jnp.float32).reshape(ROWS, HEADS, HD)
    placing = (admit_slot[None, :] == jnp.arange(ROWS, dtype=jnp.int32)[:, None]).astype(jnp.float32)
    taken_slots = lax.optimization_barrier(jnp.sum(placing, axis=1)) > 0.5
    kept_slots = occupancy.astype(jnp.float32)
    picked = jnp.einsum('ra,rhk->ahk', placing, query_rows, precision=exact_mode)
    arrived = jnp.einsum('ahk,ahkv->ahv', picked, incoming_state, precision=exact_mode)
    from_new = jnp.einsum('ra,ahv->rhv', placing, arrived, precision=exact_mode)
    from_old = jnp.einsum('rhk,rhkv->rhv', query_rows, cached_state, precision=exact_mode) * kept_slots[:, None, None]
    base_product = jnp.where(taken_slots[:, None, None], from_new, from_old)
    self_score = lax.optimization_barrier(jnp.sum(query_rows * key_rows, axis=2))
    raw_output = jnp.exp(-decay_rate)[None, :, None] * base_product + self_score[:, :, None] * value_rows
    scaled = raw_output * lax.rsqrt(lax.optimization_barrier(jnp.mean(raw_output * raw_output, axis=2, keepdims=True)) + epsilon)
    head_out = scaled.astype(jnp.bfloat16).reshape(ROWS, HEADS * HD)
    attended = jnp.dot(head_out, out_proj, preferred_element_type=jnp.float32)
    mixed_rows = (residual_in.astype(jnp.float32) + attended).astype(jnp.bfloat16)
    mixed_wide = mixed_rows.astype(jnp.float32)
    row_power = lax.optimization_barrier(jnp.mean(mixed_wide * mixed_wide, axis=1, keepdims=True))
    normed = (mixed_wide * lax.rsqrt(row_power + epsilon) * norm_gain[None, :]).astype(jnp.bfloat16)
    normed_wide = normed.astype(jnp.float32)
    split_count = PIECES // EXPERTS
    gate_all = gate_proj.reshape(EXPERTS, split_count, D, FF // split_count)
    up_all = up_proj.reshape(EXPERTS, split_count, D, FF // split_count)
    down_all = down_proj.reshape(EXPERTS, FF, D)
    slot_index = jnp.arange(CAP, dtype=jnp.int32)

    def one_expert(running, expert):
        route_hit = routes == expert
        named_rows = jnp.any(route_hit, axis=1)
        weight = lax.optimization_barrier(jnp.sum(jnp.where(route_hit, route_weight, 0.0), axis=1))
        position = jnp.cumsum(named_rows.astype(jnp.int32)) - 1
        chosen = (named_rows[None, :] & (position[None, :] == slot_index[:, None])).astype(jnp.float32)
        rows_input = jnp.dot(chosen, normed_wide, precision=exact_mode)
        gate_piece = lax.dynamic_index_in_dim(gate_all, expert, 0, keepdims=False).astype(jnp.float32)
        up_piece = lax.dynamic_index_in_dim(up_all, expert, 0, keepdims=False).astype(jnp.float32)
        gate_value = jnp.einsum('kd,sdf->ksf', rows_input, gate_piece, precision=exact_mode).reshape(CAP, FF)
        up_value = jnp.einsum('kd,sdf->ksf', rows_input, up_piece, precision=exact_mode).reshape(CAP, FF)
        hidden = (jax.nn.silu(gate_value) * up_value).astype(jnp.bfloat16)
        down_piece = lax.dynamic_index_in_dim(down_all, expert, 0, keepdims=False)
        output = jnp.dot(hidden, down_piece, preferred_element_type=jnp.float32)
        running = running + jnp.dot((chosen * weight[None, :]).T, output, precision=exact_mode)
        return (running, None)
    routed_sum, _ = lax.scan(one_expert, jnp.zeros((ROWS, D), jnp.float32), jnp.arange(EXPERTS, dtype=jnp.int32))
    return (mixed_wide + routed_sum).astype(jnp.bfloat16)
```

```python
import functools

import jax
import jax.numpy as jnp
from jax import lax
from jax.experimental import pallas as pl
from jax.experimental.pallas import tpu as pltpu
from jax.sharding import PartitionSpec as P

EPSILON = 1e-06
CORES = 2
CAPACITY = 32
MESH = pl.DeviceIdType.MESH
F32 = jnp.float32
BF16 = jnp.bfloat16
GRID = (4, 4, 8)


def iota(shape, dim):
    return lax.broadcasted_iota(jnp.int32, shape, dim)


def natural_row(position, grid):
    _, ny, nz = grid
    pair = 2 * CORES
    block = ny * pair
    zi = position // block
    yi = (position % block) // pair
    return yi * (nz * pair) + zi * pair + position % pair


def dot(a, b, dims=((1,), (0,)), precision=None):
    return lax.dot_general(a, b, (dims, ((), ())), preferred_element_type=F32, precision=precision)


def layer_kernel(
    grid,
    admit_ref,
    residual_ref,
    q_ref,
    k_ref,
    v_ref,
    arrived_ref,
    occupancy_ref,
    decay_ref,
    gain_ref,
    routes_ref,
    weight_ref,
    state_hbm,
    wo_hbm,
    gate_hbm,
    up_hbm,
    down_hbm,
    out_ref,
    state_v,
    wo_v,
    gate_v,
    up_v,
    down_v,
    heads_buf,
    partial,
    snd3,
    rcv3,
    own4,
    snd4,
    rcv4,
    snd5,
    rcv5,
    full,
    snd7,
    xin,
    snd8,
    rcv8,
    own9,
    snd9,
    rcv9,
    snd10,
    rcv10,
    local_sem,
    s2,
    r2,
    s3,
    r3,
    s4,
    r4,
    s5,
    r5,
    s6,
    r6,
    s7,
    r7,
    s8,
    r8,
    s9,
    r9,
    s10,
    r10,
):
    nx, ny, nz = grid
    slots = q_ref.shape[0]
    hd = q_ref.shape[1]
    rows = nx * slots
    rz = rows // nz
    cols = xin.shape[2]
    admitted = admit_ref.shape[0]

    x = lax.axis_index("sec")
    ep = lax.axis_index("ep")
    c = lax.rem(ep, CORES)
    z = lax.rem(ep // CORES, nz)
    y = ep // (CORES * nz)

    def at(xx, yy, zz, cc):
        return (xx, (yy * nz + zz) * CORES + cc)

    loads = [
        pltpu.make_async_copy(src, dst, local_sem.at[i])
        for i, (src, dst) in enumerate(
            (
                (state_hbm, state_v),
                (wo_hbm, wo_v),
                (gate_hbm, gate_v),
                (up_hbm, up_v),
                (down_hbm, down_v),
            )
        )
    ]
    for load in loads:
        load.start()

    barrier = pltpu.get_barrier_semaphore()
    partners = []
    for i in range(1, nx * ny):
        partners.append(at(lax.rem(x + i // ny, nx), lax.rem(y + i % ny, ny), z, c))
    for dz in range(1, nz):
        partners.append(at(x, y, lax.rem(z + dz, nz), c))
    for dy in range(ny):
        partners.append(at(x, lax.rem(y + dy, ny), z, 1 - c))
    for partner in partners:
        pl.semaphore_signal(barrier, inc=1, device_id=partner, device_id_type=MESH)

    q = q_ref[...].astype(F32)
    kk = k_ref[...].astype(F32)
    vv = v_ref[...].astype(F32)
    occupancy = occupancy_ref[...].astype(F32)
    eye = iota((slots, slots), 0) == iota((slots, slots), 1)
    kept = jnp.sum(jnp.where(eye, occupancy, 0.0), axis=1, keepdims=True)
    slot_row = iota((slots, 1), 0)
    taken = jnp.zeros((slots, 1), jnp.bool_)
    kb = hd // (ny * nz * CORES)
    wide = arrived_ref.shape[0]
    lane = iota((1, wide), 1)
    lane_request = (lane // kb) % admitted
    lane_slot = jnp.zeros((1, wide), jnp.int32)
    for a in range(admitted):
        slot = admit_ref[a] - x * slots
        taken = jnp.logical_or(taken, slot_row == slot)
        lane_slot = jnp.where(lane_request == a, slot, lane_slot)
    old_q = jnp.where(taken, 0.0, q * kept)
    lane2 = iota((hd, wide), 1)
    spread_key = (lane2 // (admitted * kb)) * kb + lane2 % kb
    repeat = (iota((hd, wide), 0) == spread_key).astype(BF16)
    new_q = dot(q.astype(BF16), repeat)
    new_q = jnp.where(slot_row == lane_slot, new_q, 0.0).astype(BF16)
    base_new = dot(new_q, arrived_ref[...])
    loads[0].wait()
    base_old = []
    row8 = iota((8, hd), 0)
    for chunk in range(slots // 8):
        part = old_q[chunk * 8 : chunk * 8 + 8]
        diagonal = jnp.concatenate(
            [jnp.where(row8 == s, part, 0.0) for s in range(8)], axis=1
        ).astype(BF16)
        states = state_v[chunk * 8 * hd : (chunk + 1) * 8 * hd, :].astype(BF16)
        base_old.append(dot(diagonal, states))
    base = jnp.concatenate(base_old, axis=0) + base_new
    raw = jnp.exp(-decay_ref[...]) * base + jnp.sum(q * kk, axis=1, keepdims=True) * vv
    power = jnp.mean(raw * raw, axis=1, keepdims=True)
    heads_buf[x] = (raw * lax.rsqrt(power + EPSILON)).astype(BF16)

    pl.semaphore_wait(barrier, len(partners))

    copies2 = []
    for dx in range(1, nx):
        copy = pltpu.make_async_remote_copy(
            heads_buf.at[x],
            heads_buf.at[x],
            s2.at[dx - 1],
            r2.at[dx - 1],
            device_id=at(lax.rem(x + dx, nx), y, z, c),
            device_id_type=MESH,
        )
        copy.start()
        copies2.append(copy)

    position0 = iota((rows, rows), 0)
    position1 = iota((rows, rows), 1)
    row_of0 = natural_row(position0, grid)
    row_of1 = natural_row(position1, grid)
    to_held = (position0 == row_of1).astype(F32)
    not_after = (row_of0 <= row_of1).astype(BF16)
    expert = iota((8, rows), 0) * (nz // 2) + z // 2
    hit = jnp.zeros((8, rows), jnp.bool_)
    weight = jnp.zeros((8, rows), F32)
    for t in range(routes_ref.shape[0]):
        route = jnp.broadcast_to(routes_ref[t : t + 1, :].astype(F32), (8, rows))
        route = dot(route.astype(BF16), to_held.astype(BF16))
        gate_value = jnp.broadcast_to(weight_ref[t : t + 1, :], (8, rows))
        gate_value = dot(gate_value, to_held, precision=lax.Precision.HIGHEST)
        same = route == expert.astype(F32)
        hit = jnp.logical_or(hit, same)
        weight = weight + jnp.where(same, gate_value, 0.0)
    rank = dot(hit.astype(F32).astype(BF16), not_after)
    rank = jnp.where(hit, rank, 0.0)
    place = (iota((CAPACITY, rows), 0) + 1).astype(F32)
    picks, slot_weights = [], []
    for yy in range(ny):
        chosen = rank[yy : yy + 1, :] == place
        picks.append(chosen.astype(F32))
        slot_weights.append(
            jnp.sum(jnp.where(chosen, weight[yy : yy + 1, :], 0.0), axis=1, keepdims=True)
        )
    pick = jnp.concatenate(picks, axis=0).astype(BF16)
    from_held = (position1 == row_of0).astype(BF16)

    loads[1].wait()
    for copy in copies2:
        copy.wait_recv()

    heads = heads_buf[...].reshape(rows, hd)
    heads = dot(from_held, heads).astype(BF16)
    first = z * rz + y * (2 * CORES) + c * 2
    group = pl.multiple_of((first // 8) * 8, 8)
    inside = first - group
    row_in_group = iota((8, cols), 0)
    for yy in range(ny):
        partial[yy] = dot(heads, wo_v[:, yy * cols : (yy + 1) * cols])
        res = residual_ref[:, yy * cols : (yy + 1) * cols].astype(F32)
        add = jnp.where(row_in_group == inside, res[0:1, :], 0.0) + jnp.where(
            row_in_group == inside + 1, res[1:2, :], 0.0
        )
        partial[yy, pl.ds(group, 8), :] += add
        snd3[yy] = partial[yy].astype(BF16)
    copies3 = []
    for dy in range(1, ny):
        to = lax.rem(y + dy, ny)
        copy = pltpu.make_async_remote_copy(
            snd3.at[to],
            rcv3.at[dy - 1],
            s3.at[dy - 1],
            r3.at[dy - 1],
            device_id=at(x, to, z, c),
            device_id_type=MESH,
        )
        copy.start()
        copies3.append(copy)
    total = partial[y]
    for i, copy in enumerate(copies3):
        copy.wait_recv()
        total = total + rcv3[i].astype(F32)

    for zz in range(nz):
        own4[zz] = total[zz * rz : (zz + 1) * rz]
        snd4[zz] = total[zz * rz : (zz + 1) * rz].astype(BF16)
    copies4 = []
    for dz in range(1, nz):
        to = lax.rem(z + dz, nz)
        copy = pltpu.make_async_remote_copy(
            snd4.at[to],
            rcv4.at[dz - 1],
            s4.at[dz - 1],
            r4.at[dz - 1],
            device_id=at(x, y, to, c),
            device_id_type=MESH,
        )
        copy.start()
        copies4.append(copy)
    mine = own4[z]
    for i, copy in enumerate(copies4):
        copy.wait_recv()
        mine = mine + rcv4[i].astype(F32)

    snd5[...] = mine
    copy5 = pltpu.make_async_remote_copy(
        snd5, rcv5, s5.at[0], r5.at[0], device_id=at(x, y, z, 1 - c), device_id_type=MESH
    )
    copy5.start()
    copy5.wait_recv()
    mixed = (mine + rcv5[...]).astype(BF16)
    full[z] = mixed

    copies6 = []
    for dz in range(1, nz):
        copy = pltpu.make_async_remote_copy(
            full.at[z],
            full.at[z],
            s6.at[dz - 1],
            r6.at[dz - 1],
            device_id=at(x, y, lax.rem(z + dz, nz), c),
            device_id_type=MESH,
        )
        copy.start()
        copies6.append(copy)
    for copy in copies6:
        copy.wait_recv()

    here = x * ny + y
    picked = dot(pick, full[...].reshape(rows, cols)).astype(BF16)
    for yy in range(ny):
        snd7[yy] = picked[yy * CAPACITY : (yy + 1) * CAPACITY]

    def to_experts(i):
        xx, yy = lax.rem(x + i // ny, nx), lax.rem(y + lax.rem(i, ny), ny)
        return pltpu.make_async_remote_copy(
            snd7.at[yy],
            xin.at[here],
            s7.at[i],
            r7.at[i],
            device_id=at(xx, yy, z, c),
            device_id_type=MESH,
        )

    @pl.loop(1, nx * ny)
    def _(i):
        to_experts(i).start()

    xin[here] = snd7[y]
    for load in loads[2:]:
        load.wait()

    def one_block(block, carry):
        gate_sum, up_sum, squares = carry
        taken_rows = xin[block].astype(F32)
        columns = pl.ds(pl.multiple_of(block * cols, cols), cols)
        squares = squares + jnp.sum(taken_rows * taken_rows, axis=1, keepdims=True)
        scaled = (taken_rows * gain_ref[:, columns]).astype(BF16)
        gate_sum = gate_sum + dot(scaled, gate_v[:, columns], ((1,), (1,)))
        up_sum = up_sum + dot(scaled, up_v[:, columns], ((1,), (1,)))
        return gate_sum, up_sum, squares

    def arriving(i, carry):
        to_experts(i).wait_recv()
        xx = lax.rem(x - i // ny + nx, nx)
        yy = lax.rem(y - lax.rem(i, ny) + ny, ny)
        return one_block(xx * ny + yy, carry)

    hidden_units = gate_v.shape[0]
    carry = (
        jnp.zeros((CAPACITY, hidden_units), F32),
        jnp.zeros((CAPACITY, hidden_units), F32),
        jnp.zeros((CAPACITY, 1), F32),
    )
    carry = one_block(here, carry)
    gate_sum, up_sum, squares = lax.fori_loop(1, nx * ny, arriving, carry)
    scale = lax.rsqrt(squares / (nx * ny * cols) + EPSILON)
    gate_sum = gate_sum * scale
    up_sum = up_sum * scale
    hidden = (gate_sum / (1.0 + jnp.exp(-gate_sum)) * up_sum).astype(BF16)

    def back(i):
        xx, yy = lax.rem(x + i // ny, nx), lax.rem(y + lax.rem(i, ny), ny)
        return pltpu.make_async_remote_copy(
            snd8.at[i],
            rcv8.at[here],
            s8.at[i],
            r8.at[i],
            device_id=at(xx, yy, z, c),
            device_id_type=MESH,
        )

    def down_block(block):
        columns = pl.ds(pl.multiple_of(block * cols, cols), cols)
        return dot(hidden, down_v[:, columns]).astype(BF16)

    @pl.loop(1, nx * ny)
    def _(i):
        xx, yy = lax.rem(x + i // ny, nx), lax.rem(y + lax.rem(i, ny), ny)
        snd8[i] = down_block(xx * ny + yy)
        back(i).start()

    rcv8[here] = down_block(here)

    @pl.loop(1, nx * ny)
    def _(i):
        back(i).wait_recv()

    summed = []
    for yy in range(ny):
        term = rcv8[yy].astype(F32)
        for xx in range(1, nx):
            term = term + rcv8[xx * ny + yy].astype(F32)
        summed.append(term * slot_weights[yy])
    summed = jnp.concatenate(summed, axis=0).astype(BF16)
    routed = dot(pick, summed, ((0,), (0,)))
    for zz in range(nz):
        own9[zz] = routed[zz * rz : (zz + 1) * rz]
        snd9[zz] = routed[zz * rz : (zz + 1) * rz].astype(BF16)
    copies9 = []
    for dz in range(1, nz):
        to = lax.rem(z + dz, nz)
        copy = pltpu.make_async_remote_copy(
            snd9.at[to],
            rcv9.at[dz - 1],
            s9.at[dz - 1],
            r9.at[dz - 1],
            device_id=at(x, y, to, c),
            device_id_type=MESH,
        )
        copy.start()
        copies9.append(copy)
    block = own9[z] + mixed.astype(F32) * jnp.where(c == 0, 1.0, 0.0)
    for i, copy in enumerate(copies9):
        copy.wait_recv()
        block = block + rcv9[i].astype(F32)

    for i in range(ny * CORES):
        snd10[i] = block[2 * i : 2 * i + 2, :]
    spot = y * CORES + c
    copies10 = []
    for i in range(1, ny * CORES):
        to_y, to_c = lax.rem(y + i // CORES, ny), lax.rem(c + i % CORES, CORES)
        copy = pltpu.make_async_remote_copy(
            snd10.at[to_y * CORES + to_c],
            rcv10.at[spot],
            s10.at[i - 1],
            r10.at[i - 1],
            device_id=at(x, to_y, z, to_c),
            device_id_type=MESH,
        )
        copy.start()
        copies10.append(copy)
    rcv10[spot] = snd10[spot]
    for copy in copies10:
        copy.wait_recv()
    for yy in range(ny):
        out_ref[:, yy * cols : (yy + 1) * cols] = (
            rcv10[yy * CORES] + rcv10[yy * CORES + 1]
        ).astype(BF16)

    for copy in copies2 + copies3 + copies4 + [copy5] + copies6 + copies9 + copies10:
        copy.wait_send()

    @pl.loop(1, nx * ny)
    def _(i):
        to_experts(i).wait_send()
        back(i).wait_send()


def body(
    grid,
    residual_in,
    queries,
    keys_new,
    values_new,
    cached_state,
    incoming_state,
    admit_slot,
    occupancy,
    decay_rate,
    out_proj,
    norm_gain,
    routes,
    route_weight,
    gate_proj,
    up_proj,
    down_proj,
):
    nx, ny, nz = grid
    slots, hd = queries.shape
    rows = nx * slots
    rz = rows // nz
    cols = residual_in.shape[1] // ny
    blocks = nx * ny
    units = gate_proj.shape[2]
    width = gate_proj.shape[1]
    admitted, heads, kb, _ = incoming_state.shape

    arrived = lax.all_to_all(
        incoming_state.astype(BF16).transpose(1, 0, 2, 3).reshape(heads, admitted * kb, hd),
        "ep",
        split_axis=0,
        concat_axis=0,
        tiled=True,
    ).reshape(heads * admitted * kb, hd)

    vmem = pl.BlockSpec(memory_space=pltpu.VMEM)
    anywhere = pl.BlockSpec(memory_space=pl.ANY)
    dma = lambda n: pltpu.SemaphoreType.DMA((n,))
    scratch = [
        pltpu.VMEM((slots * hd, hd), F32),
        pltpu.VMEM(out_proj.shape, BF16),
        pltpu.VMEM((units, width), BF16),
        pltpu.VMEM((units, width), BF16),
        pltpu.VMEM((units, width), BF16),
        pltpu.VMEM((nx, slots, hd), BF16),
        pltpu.VMEM((ny, rows, cols), F32),
        pltpu.VMEM((ny, rows, cols), BF16),
        pltpu.VMEM((ny - 1, rows, cols), BF16),
        pltpu.VMEM((nz, rz, cols), F32),
        pltpu.VMEM((nz, rz, cols), BF16),
        pltpu.VMEM((nz - 1, rz, cols), BF16),
        pltpu.VMEM((rz, cols), F32),
        pltpu.VMEM((rz, cols), F32),
        pltpu.VMEM((nz, rz, cols), BF16),
        pltpu.VMEM((ny, CAPACITY, cols), BF16),
        pltpu.VMEM((blocks, CAPACITY, cols), BF16),
        pltpu.VMEM((blocks, CAPACITY, cols), BF16),
        pltpu.VMEM((blocks, CAPACITY, cols), BF16),
        pltpu.VMEM((nz, rz, cols), F32),
        pltpu.VMEM((nz, rz, cols), BF16),
        pltpu.VMEM((nz - 1, rz, cols), BF16),
        pltpu.VMEM((ny * CORES, 2, cols), F32),
        pltpu.VMEM((ny * CORES, 2, cols), F32),
        dma(5),
    ]
    for n in (nx - 1, ny - 1, nz - 1, 1, nz - 1, blocks, blocks, nz - 1, ny * CORES - 1):
        scratch += [dma(n), dma(n)]

    return pl.pallas_call(
        functools.partial(layer_kernel, grid),
        out_shape=jax.ShapeDtypeStruct(residual_in.shape, BF16),
        in_specs=[pl.BlockSpec(memory_space=pltpu.SMEM)] + [vmem] * 10 + [anywhere] * 5,
        out_specs=vmem,
        scratch_shapes=scratch,
        compiler_params=pltpu.CompilerParams(
            collective_id=0, has_side_effects=True, vmem_limit_bytes=48 * 2**20
        ),
    )(
        admit_slot,
        residual_in,
        queries,
        keys_new,
        values_new,
        arrived,
        occupancy.reshape(1, slots),
        decay_rate.reshape(1, 1),
        norm_gain.reshape(1, width),
        routes.T,
        route_weight.T,
        cached_state.reshape(slots * hd, hd),
        out_proj,
        gate_proj[0].T,
        up_proj[0].T,
        down_proj[0],
    )


def solution(mesh):
    in_specs = (
        P("ep", "sec"),
        P("sec", "ep"),
        P("sec", "ep"),
        P("sec", "ep"),
        P("sec", "ep", None, None),
        P("sec", None, "ep", None),
        P("sec"),
        P("sec"),
        P("ep"),
        P("ep", "sec"),
        P(),
        P(),
        P(),
        P("ep", None, "sec"),
        P("ep", None, "sec"),
        P("ep", "sec", None),
    )
    return jax.shard_map(
        functools.partial(body, GRID),
        mesh=mesh,
        in_specs=in_specs,
        out_specs=P("ep", "sec"),
        check_vma=False,
    )
```

```python
import functools

import jax
import jax.numpy as jnp
from jax import lax
from jax.experimental import pallas as pl
from jax.experimental.pallas import tpu as pltpu
from jax.sharding import PartitionSpec as P

EPSILON = 1e-06
CORES = 2
CAPACITY = 32
VMEM_BYTES = 62 * 2**20
MESH = pl.DeviceIdType.MESH
F32 = jnp.float32
BF16 = jnp.bfloat16
GRID = (4, 4, 8)


def iota(shape, dim):
    return lax.broadcasted_iota(jnp.int32, shape, dim)


def natural_row(position, grid):
    _, ny, nz = grid
    pair = 2 * CORES
    block = ny * pair
    zi = position // block
    yi = (position % block) // pair
    return yi * (nz * pair) + zi * pair + position % pair


def dot(a, b, dims=((1,), (0,)), precision=None):
    return lax.dot_general(a, b, (dims, ((), ())), preferred_element_type=F32, precision=precision)


def layer_kernel(
    grid,
    operands,
    out_ref,
    incoming_v,
    admit_ref,
    occupancy_ref,
    q_ref,
    k_ref,
    v_ref,
    decay_ref,
    routes_ref,
    weight_ref,
    residual_ref,
    gain_ref,
    state_v,
    wo_v,
    gate_v,
    up_v,
    down_v,
    snd1,
    rcv1,
    heads_buf,
    partial,
    snd3,
    rcv3,
    own4,
    snd4,
    rcv4,
    snd5,
    rcv5,
    full,
    snd7,
    xin,
    snd8,
    rcv8,
    own9,
    snd9,
    rcv9,
    snd10,
    rcv10,
    local_sem,
    s1,
    r1,
    s2,
    r2,
    s3,
    r3,
    s4,
    r4,
    s5,
    r5,
    s6,
    r6,
    s7,
    r7,
    s8,
    r8,
    s9,
    r9,
    s10,
    r10,
):
    nx, ny, nz = grid
    slots, hd = q_ref.shape
    parts = ny * nz * CORES
    kb = hd // parts
    rows = nx * slots
    rz = rows // nz
    cols = xin.shape[2]
    admitted = admit_ref.shape[0]
    wide = parts * admitted * kb

    x = lax.axis_index("sec")
    ep = lax.axis_index("ep")
    c = lax.rem(ep, CORES)
    z = lax.rem(ep // CORES, nz)
    y = ep // (CORES * nz)

    def at(xx, yy, zz, cc):
        return (xx, (yy * nz + zz) * CORES + cc)

    incoming_hbm, *others = operands
    held = (
        admit_ref,
        occupancy_ref,
        q_ref,
        k_ref,
        v_ref,
        decay_ref,
        state_v,
        routes_ref,
        weight_ref,
        residual_ref,
        wo_v,
        gain_ref,
        gate_v,
        up_v,
        down_v,
    )
    incoming_loads = [
        pltpu.make_async_copy(
            incoming_hbm.at[a], incoming_v.at[:, kb * a : kb * (a + 1), :], local_sem.at[a]
        )
        for a in range(admitted)
    ]
    loads = [
        pltpu.make_async_copy(src, dst, local_sem.at[admitted + i])
        for i, (src, dst) in enumerate(zip(others, held))
    ]
    for load in incoming_loads + loads:
        load.start()

    barrier = pltpu.get_barrier_semaphore()

    @pl.loop(1, parts)
    def _(i):
        pl.semaphore_signal(
            barrier, inc=1, device_id=(x, lax.rem(ep + i, parts)), device_id_type=MESH
        )

    @pl.loop(ny, nx * ny)
    def _(i):
        partner = at(lax.rem(x + i // ny, nx), lax.rem(y + lax.rem(i, ny), ny), z, c)
        pl.semaphore_signal(barrier, inc=1, device_id=partner, device_id_type=MESH)

    for load in incoming_loads:
        load.wait()
    snd1[...] = incoming_v[...].astype(BF16)
    pl.semaphore_wait(barrier, parts - 1 + (nx - 1) * ny)

    @pl.loop(1, parts)
    def _(i):
        to = lax.rem(ep + i, parts)
        pltpu.make_async_remote_copy(
            snd1.at[to],
            rcv1.at[ep],
            s1.at[0],
            r1.at[0],
            device_id=(x, to),
            device_id_type=MESH,
        ).start()

    rcv1[ep] = snd1[ep]
    every1 = pltpu.make_async_remote_copy(
        snd1.at[pl.ds(0, parts - 1)],
        rcv1.at[pl.ds(0, parts - 1)],
        s1.at[0],
        r1.at[0],
        device_id=(x, lax.rem(ep + 1, parts)),
        device_id_type=MESH,
    )

    for load in loads[:7]:
        load.wait()

    q = q_ref[...].astype(F32)
    kk = k_ref[...].astype(F32)
    vv = v_ref[...].astype(F32)
    occupancy = occupancy_ref[...].astype(F32)
    eye = iota((slots, slots), 0) == iota((slots, slots), 1)
    kept = jnp.sum(jnp.where(eye, occupancy, 0.0), axis=1, keepdims=True)
    slot_row = iota((slots, 1), 0)
    taken = jnp.zeros((slots, 1), jnp.bool_)
    lane = iota((1, wide), 1)
    lane_request = (lane // kb) % admitted
    lane_slot = jnp.zeros((1, wide), jnp.int32)
    for a in range(admitted):
        slot = admit_ref[a] - x * slots
        taken = jnp.logical_or(taken, slot_row == slot)
        lane_slot = jnp.where(lane_request == a, slot, lane_slot)
    old_q = jnp.where(taken, 0.0, q * kept)
    lane2 = iota((hd, wide), 1)
    spread_key = (lane2 // (admitted * kb)) * kb + lane2 % kb
    repeat = (iota((hd, wide), 0) == spread_key).astype(BF16)
    new_q = dot(q.astype(BF16), repeat)
    new_q = jnp.where(slot_row == lane_slot, new_q, 0.0).astype(BF16)
    base_old = []
    row8 = iota((8, hd), 0)
    for chunk in range(slots // 8):
        part = old_q[chunk * 8 : chunk * 8 + 8]
        diagonal = jnp.concatenate(
            [jnp.where(row8 == s, part, 0.0) for s in range(8)], axis=1
        ).astype(BF16)
        states = state_v[chunk * 8 * hd : (chunk + 1) * 8 * hd, :].astype(BF16)
        base_old.append(dot(diagonal, states))
    every1.wait_recv()
    arrived = rcv1[...].astype(F32).reshape(wide, hd).astype(BF16)
    base = jnp.concatenate(base_old, axis=0) + dot(new_q, arrived)
    raw = jnp.exp(-decay_ref[...]) * base + jnp.sum(q * kk, axis=1, keepdims=True) * vv
    power = jnp.mean(raw * raw, axis=1, keepdims=True)
    heads_buf[x] = (raw * lax.rsqrt(power + EPSILON)).astype(BF16)

    copies2 = []
    for dx in range(1, nx):
        copy = pltpu.make_async_remote_copy(
            heads_buf.at[x],
            heads_buf.at[x],
            s2.at[dx - 1],
            r2.at[dx - 1],
            device_id=at(lax.rem(x + dx, nx), y, z, c),
            device_id_type=MESH,
        )
        copy.start()
        copies2.append(copy)

    for load in loads[7:9]:
        load.wait()

    position0 = iota((rows, rows), 0)
    position1 = iota((rows, rows), 1)
    row_of0 = natural_row(position0, grid)
    row_of1 = natural_row(position1, grid)
    to_held = (position0 == row_of1).astype(F32)
    not_after = (row_of0 <= row_of1).astype(BF16)
    expert = iota((8, rows), 0) * (nz // 2) + z // 2
    hit = jnp.zeros((8, rows), jnp.bool_)
    weight = jnp.zeros((8, rows), F32)
    for t in range(routes_ref.shape[0]):
        route = jnp.broadcast_to(routes_ref[t : t + 1, :].astype(F32), (8, rows))
        route = dot(route.astype(BF16), to_held.astype(BF16))
        gate_value = jnp.broadcast_to(weight_ref[t : t + 1, :], (8, rows))
        gate_value = dot(gate_value, to_held, precision=lax.Precision.HIGHEST)
        same = route == expert.astype(F32)
        hit = jnp.logical_or(hit, same)
        weight = weight + jnp.where(same, gate_value, 0.0)
    rank = dot(hit.astype(F32).astype(BF16), not_after)
    rank = jnp.where(hit, rank, 0.0)
    place = (iota((CAPACITY, rows), 0) + 1).astype(F32)
    picks, slot_weights = [], []
    for yy in range(ny):
        chosen = rank[yy : yy + 1, :] == place
        picks.append(chosen.astype(F32))
        slot_weights.append(
            jnp.sum(jnp.where(chosen, weight[yy : yy + 1, :], 0.0), axis=1, keepdims=True)
        )
    pick = jnp.concatenate(picks, axis=0).astype(BF16)
    from_held = (position1 == row_of0).astype(BF16)

    for load in loads[9:12]:
        load.wait()
    for copy in copies2:
        copy.wait_recv()

    heads = heads_buf[...].reshape(rows, hd)
    heads = dot(from_held, heads).astype(BF16)
    first = z * rz + y * (2 * CORES) + c * 2
    group = pl.multiple_of((first // 8) * 8, 8)
    inside = first - group
    row_in_group = iota((8, cols), 0)
    for yy in range(ny):
        partial[yy] = dot(heads, wo_v[:, yy * cols : (yy + 1) * cols])
        res = residual_ref[:, yy * cols : (yy + 1) * cols].astype(F32)
        add = jnp.where(row_in_group == inside, res[0:1, :], 0.0) + jnp.where(
            row_in_group == inside + 1, res[1:2, :], 0.0
        )
        partial[yy, pl.ds(group, 8), :] += add
        snd3[yy] = partial[yy].astype(BF16)
    copies3 = []
    for dy in range(1, ny):
        to = lax.rem(y + dy, ny)
        copy = pltpu.make_async_remote_copy(
            snd3.at[to],
            rcv3.at[dy - 1],
            s3.at[dy - 1],
            r3.at[dy - 1],
            device_id=at(x, to, z, c),
            device_id_type=MESH,
        )
        copy.start()
        copies3.append(copy)
    total = partial[y]
    for i, copy in enumerate(copies3):
        copy.wait_recv()
        total = total + rcv3[i].astype(F32)

    for zz in range(nz):
        own4[zz] = total[zz * rz : (zz + 1) * rz]
        snd4[zz] = total[zz * rz : (zz + 1) * rz].astype(BF16)
    copies4 = []
    for dz in range(1, nz):
        to = lax.rem(z + dz, nz)
        copy = pltpu.make_async_remote_copy(
            snd4.at[to],
            rcv4.at[dz - 1],
            s4.at[dz - 1],
            r4.at[dz - 1],
            device_id=at(x, y, to, c),
            device_id_type=MESH,
        )
        copy.start()
        copies4.append(copy)
    mine = own4[z]
    for i, copy in enumerate(copies4):
        copy.wait_recv()
        mine = mine + rcv4[i].astype(F32)

    snd5[...] = mine
    copy5 = pltpu.make_async_remote_copy(
        snd5, rcv5, s5.at[0], r5.at[0], device_id=at(x, y, z, 1 - c), device_id_type=MESH
    )
    copy5.start()
    copy5.wait_recv()
    mixed = (mine + rcv5[...]).astype(BF16)
    full[z] = mixed

    copies6 = []
    for dz in range(1, nz):
        copy = pltpu.make_async_remote_copy(
            full.at[z],
            full.at[z],
            s6.at[dz - 1],
            r6.at[dz - 1],
            device_id=at(x, y, lax.rem(z + dz, nz), c),
            device_id_type=MESH,
        )
        copy.start()
        copies6.append(copy)
    for copy in copies6:
        copy.wait_recv()

    here = x * ny + y
    picked = dot(pick, full[...].reshape(rows, cols)).astype(BF16)
    for yy in range(ny):
        snd7[yy] = picked[yy * CAPACITY : (yy + 1) * CAPACITY]

    def to_experts(i):
        xx, yy = lax.rem(x + i // ny, nx), lax.rem(y + lax.rem(i, ny), ny)
        return pltpu.make_async_remote_copy(
            snd7.at[yy],
            xin.at[here],
            s7.at[i],
            r7.at[i],
            device_id=at(xx, yy, z, c),
            device_id_type=MESH,
        )

    @pl.loop(1, nx * ny)
    def _(i):
        to_experts(i).start()

    xin[here] = snd7[y]
    for load in loads[12:]:
        load.wait()

    def one_block(block, carry):
        gate_sum, up_sum, squares = carry
        taken_rows = xin[block].astype(F32)
        columns = pl.ds(pl.multiple_of(block * cols, cols), cols)
        squares = squares + jnp.sum(taken_rows * taken_rows, axis=1, keepdims=True)
        scaled = (taken_rows * gain_ref[:, columns]).astype(BF16)
        gate_sum = gate_sum + dot(scaled, gate_v[:, columns], ((1,), (1,)))
        up_sum = up_sum + dot(scaled, up_v[:, columns], ((1,), (1,)))
        return gate_sum, up_sum, squares

    def arriving(i, carry):
        to_experts(i).wait_recv()
        xx = lax.rem(x - i // ny + nx, nx)
        yy = lax.rem(y - lax.rem(i, ny) + ny, ny)
        return one_block(xx * ny + yy, carry)

    hidden_units = gate_v.shape[0]
    carry = (
        jnp.zeros((CAPACITY, hidden_units), F32),
        jnp.zeros((CAPACITY, hidden_units), F32),
        jnp.zeros((CAPACITY, 1), F32),
    )
    carry = one_block(here, carry)
    gate_sum, up_sum, squares = lax.fori_loop(1, nx * ny, arriving, carry)
    scale = lax.rsqrt(squares / (nx * ny * cols) + EPSILON)
    gate_sum = gate_sum * scale
    up_sum = up_sum * scale
    hidden = (gate_sum / (1.0 + jnp.exp(-gate_sum)) * up_sum).astype(BF16)

    def back(i):
        xx, yy = lax.rem(x + i // ny, nx), lax.rem(y + lax.rem(i, ny), ny)
        return pltpu.make_async_remote_copy(
            snd8.at[i],
            rcv8.at[here],
            s8.at[i],
            r8.at[i],
            device_id=at(xx, yy, z, c),
            device_id_type=MESH,
        )

    def down_block(block):
        columns = pl.ds(pl.multiple_of(block * cols, cols), cols)
        return dot(hidden, down_v[:, columns]).astype(BF16)

    @pl.loop(1, nx * ny)
    def _(i):
        xx, yy = lax.rem(x + i // ny, nx), lax.rem(y + lax.rem(i, ny), ny)
        snd8[i] = down_block(xx * ny + yy)
        back(i).start()

    rcv8[here] = down_block(here)

    @pl.loop(1, nx * ny)
    def _(i):
        back(i).wait_recv()

    summed = []
    for yy in range(ny):
        term = rcv8[yy].astype(F32)
        for xx in range(1, nx):
            term = term + rcv8[xx * ny + yy].astype(F32)
        summed.append(term * slot_weights[yy])
    summed = jnp.concatenate(summed, axis=0).astype(BF16)
    routed = dot(pick, summed, ((0,), (0,)))
    for zz in range(nz):
        own9[zz] = routed[zz * rz : (zz + 1) * rz]
        snd9[zz] = routed[zz * rz : (zz + 1) * rz].astype(BF16)
    copies9 = []
    for dz in range(1, nz):
        to = lax.rem(z + dz, nz)
        copy = pltpu.make_async_remote_copy(
            snd9.at[to],
            rcv9.at[dz - 1],
            s9.at[dz - 1],
            r9.at[dz - 1],
            device_id=at(x, y, to, c),
            device_id_type=MESH,
        )
        copy.start()
        copies9.append(copy)
    block = own9[z] + mixed.astype(F32) * jnp.where(c == 0, 1.0, 0.0)
    for i, copy in enumerate(copies9):
        copy.wait_recv()
        block = block + rcv9[i].astype(F32)

    for i in range(ny * CORES):
        snd10[i] = block[2 * i : 2 * i + 2, :]
    spot = y * CORES + c
    copies10 = []
    for i in range(1, ny * CORES):
        to_y, to_c = lax.rem(y + i // CORES, ny), lax.rem(c + i % CORES, CORES)
        copy = pltpu.make_async_remote_copy(
            snd10.at[to_y * CORES + to_c],
            rcv10.at[spot],
            s10.at[i - 1],
            r10.at[i - 1],
            device_id=at(x, to_y, z, to_c),
            device_id_type=MESH,
        )
        copy.start()
        copies10.append(copy)
    rcv10[spot] = snd10[spot]
    for copy in copies10:
        copy.wait_recv()
    for yy in range(ny):
        out_ref[:, yy * cols : (yy + 1) * cols] = (
            rcv10[yy * CORES] + rcv10[yy * CORES + 1]
        ).astype(BF16)

    every1.wait_send()
    for copy in copies2 + copies3 + copies4 + [copy5] + copies6 + copies9 + copies10:
        copy.wait_send()

    @pl.loop(1, nx * ny)
    def _(i):
        to_experts(i).wait_send()
        back(i).wait_send()


def body(
    grid,
    residual_in,
    queries,
    keys_new,
    values_new,
    cached_state,
    incoming_state,
    admit_slot,
    occupancy,
    decay_rate,
    out_proj,
    norm_gain,
    routes,
    route_weight,
    gate_proj,
    up_proj,
    down_proj,
):
    nx, ny, nz = grid
    slots, hd = queries.shape
    rows = nx * slots
    rz = rows // nz
    cols = residual_in.shape[1] // ny
    blocks = nx * ny
    units = gate_proj.shape[2]
    width = gate_proj.shape[1]
    admitted, parts, kb, _ = incoming_state.shape

    vmem = pl.BlockSpec(memory_space=pltpu.VMEM)
    anywhere = pl.BlockSpec(memory_space=pl.ANY)
    dma = lambda n: pltpu.SemaphoreType.DMA((n,))
    scratch = [
        pltpu.VMEM((parts, admitted * kb, hd), F32),
        pltpu.SMEM(admit_slot.shape, jnp.int32),
        pltpu.VMEM((1, slots), jnp.int32),
        pltpu.VMEM((slots, hd), BF16),
        pltpu.VMEM((slots, hd), BF16),
        pltpu.VMEM((slots, hd), BF16),
        pltpu.VMEM((1, 1), F32),
        pltpu.VMEM((routes.shape[1], rows), jnp.int32),
        pltpu.VMEM((routes.shape[1], rows), F32),
        pltpu.VMEM(residual_in.shape, BF16),
        pltpu.VMEM((1, width), F32),
        pltpu.VMEM((slots * hd, hd), F32),
        pltpu.VMEM(out_proj.shape, BF16),
        pltpu.VMEM((units, width), BF16),
        pltpu.VMEM((units, width), BF16),
        pltpu.VMEM((units, width), BF16),
        pltpu.VMEM((parts, admitted * kb, hd), BF16),
        pltpu.VMEM((parts, admitted * kb, hd), BF16),
        pltpu.VMEM((nx, slots, hd), BF16),
        pltpu.VMEM((ny, rows, cols), F32),
        pltpu.VMEM((ny, rows, cols), BF16),
        pltpu.VMEM((ny - 1, rows, cols), BF16),
        pltpu.VMEM((nz, rz, cols), F32),
        pltpu.VMEM((nz, rz, cols), BF16),
        pltpu.VMEM((nz - 1, rz, cols), BF16),
        pltpu.VMEM((rz, cols), F32),
        pltpu.VMEM((rz, cols), F32),
        pltpu.VMEM((nz, rz, cols), BF16),
        pltpu.VMEM((ny, CAPACITY, cols), BF16),
        pltpu.VMEM((blocks, CAPACITY, cols), BF16),
        pltpu.VMEM((blocks, CAPACITY, cols), BF16),
        pltpu.VMEM((blocks, CAPACITY, cols), BF16),
        pltpu.VMEM((nz, rz, cols), F32),
        pltpu.VMEM((nz, rz, cols), BF16),
        pltpu.VMEM((nz - 1, rz, cols), BF16),
        pltpu.VMEM((ny * CORES, 2, cols), F32),
        pltpu.VMEM((ny * CORES, 2, cols), F32),
        dma(admitted + 15),
    ]
    for n in (1, nx - 1, ny - 1, nz - 1, 1, nz - 1, blocks, blocks, nz - 1, ny * CORES - 1):
        scratch += [dma(n), dma(n)]

    def kernel(*refs):
        layer_kernel(grid, refs[:16], *refs[16:])

    return pl.pallas_call(
        kernel,
        out_shape=jax.ShapeDtypeStruct(residual_in.shape, BF16),
        in_specs=[anywhere] * 16,
        out_specs=vmem,
        scratch_shapes=scratch,
        compiler_params=pltpu.CompilerParams(
            collective_id=0, has_side_effects=True, vmem_limit_bytes=VMEM_BYTES
        ),
    )(
        incoming_state,
        admit_slot,
        occupancy.reshape(1, slots),
        queries,
        keys_new,
        values_new,
        decay_rate.reshape(1, 1),
        cached_state.reshape(slots * hd, hd),
        routes.T,
        route_weight.T,
        residual_in,
        out_proj,
        norm_gain.reshape(1, width),
        gate_proj[0].T,
        up_proj[0].T,
        down_proj[0],
    )


def solution(mesh):
    in_specs = (
        P("ep", "sec"),
        P("sec", "ep"),
        P("sec", "ep"),
        P("sec", "ep"),
        P("sec", "ep", None, None),
        P("sec", None, "ep", None),
        P("sec"),
        P("sec"),
        P("ep"),
        P("ep", "sec"),
        P(),
        P(),
        P(),
        P("ep", None, "sec"),
        P("ep", None, "sec"),
        P("ep", "sec", None),
    )
    return jax.shard_map(
        functools.partial(body, GRID),
        mesh=mesh,
        in_specs=in_specs,
        out_specs=P("ep", "sec"),
        check_vma=False,
    )
```

```python
import functools

import jax
import jax.numpy as jnp
from jax import lax
from jax.experimental import pallas as pl
from jax.experimental.pallas import tpu as pltpu
from jax.sharding import PartitionSpec as P

EPSILON = 1e-06
CORES = 2
CAPACITY = 32
VMEM_BYTES = 62 * 2**20
MESH = pl.DeviceIdType.MESH
F32 = jnp.float32
BF16 = jnp.bfloat16
GRID = (4, 4, 8)


def iota(shape, dim):
    return lax.broadcasted_iota(jnp.int32, shape, dim)


def natural_row(position, grid):
    _, ny, nz = grid
    half = 2 * ny
    zi = position // (CORES * half)
    ci = (position // half) % CORES
    yi = (position % half) // 2
    return (yi * nz + zi) * (2 * CORES) + ci * 2 + position % 2


def far_first(*sizes):
    steps = [()]
    for size in sizes:
        steps = [step + (i,) for step in steps for i in range(size)]

    def distance(step):
        return sum(min(i, size - i) for i, size in zip(step, sizes))

    return sorted(steps, key=lambda step: -distance(step))[:-1]


def dot(a, b, dims=((1,), (0,)), precision=None):
    return lax.dot_general(a, b, (dims, ((), ())), preferred_element_type=F32, precision=precision)


def layer_kernel(
    grid,
    operands,
    out_ref,
    incoming_v,
    admit_ref,
    occupancy_ref,
    q_ref,
    k_ref,
    v_ref,
    decay_ref,
    routes_ref,
    weight_ref,
    residual_ref,
    gain_ref,
    state_v,
    wo_v,
    gate_v,
    up_v,
    down_v,
    snd1,
    pair1,
    rcv1,
    heads_buf,
    partial,
    snd3,
    rcv3,
    snd4,
    rcv4,
    full,
    snd7,
    xin,
    snd8,
    rcv8,
    own9,
    snd9,
    rcv9,
    snd10,
    rcv10,
    local_sem,
    s0,
    r0,
    s1,
    r1,
    s2,
    r2,
    s3,
    r3,
    s4,
    r4,
    s5,
    r5,
    s6,
    r6,
    s7,
    r7,
    s8,
    r8,
    s9,
    r9,
    s10,
    r10,
):
    nx, ny, nz = grid
    slots, hd = q_ref.shape
    parts = ny * nz * CORES
    kb = hd // parts
    rows = nx * slots
    half = 2 * ny
    plane = ny * nz
    cols = xin.shape[2]
    admitted = admit_ref.shape[0]
    wide = parts * admitted * kb

    x = lax.axis_index("sec")
    ep = lax.axis_index("ep")
    c = lax.rem(ep, CORES)
    z = lax.rem(ep // CORES, nz)
    y = ep // (CORES * nz)

    here = x * ny + y
    place_yz = y * nz + z

    def at(xx, yy, zz, cc):
        return (xx, (yy * nz + zz) * CORES + cc)

    def remote(src, dst, send_sem, recv_sem, device):
        return pltpu.make_async_remote_copy(
            src, dst, send_sem, recv_sem, device_id=device, device_id_type=MESH
        )

    def step(start, by, size):
        return lax.rem(start + by, size)

    other = at(x, y, z, 1 - c)
    in_plane = [(step(y, dy, ny), step(z, dz, nz)) for dy, dz in far_first(ny, nz)]
    in_column = [step(z, dz, nz) for (dz,) in far_first(nz)]
    in_row = [step(x, dx, nx) for (dx,) in far_first(nx)]
    steps_xy = far_first(nx, ny)

    def all_of(src, dst, send_sem, recv_sem):
        count = plane - 1
        return remote(
            src.at[pl.ds(0, count)], dst.at[pl.ds(0, count)], send_sem, recv_sem, other
        )

    incoming_hbm, *others = operands
    held = (
        admit_ref,
        occupancy_ref,
        q_ref,
        k_ref,
        v_ref,
        decay_ref,
        state_v,
        routes_ref,
        weight_ref,
        residual_ref,
        wo_v,
        gain_ref,
        gate_v,
        up_v,
        down_v,
    )
    incoming_loads = [
        pltpu.make_async_copy(
            incoming_hbm.at[a], incoming_v.at[:, kb * a : kb * (a + 1), :], local_sem.at[a]
        )
        for a in range(admitted)
    ]
    loads = [
        pltpu.make_async_copy(src, dst, local_sem.at[admitted + i])
        for i, (src, dst) in enumerate(zip(others, held))
    ]
    for load in incoming_loads + loads:
        load.start()

    barrier = pltpu.get_barrier_semaphore()
    partners = [at(x, yy, zz, c) for yy, zz in in_plane] + [other]
    partners += [
        at(step(x, dx, nx), step(y, dy, ny), z, c) for dx, dy in far_first(nx, ny) if dx
    ]
    for partner in partners:
        pl.semaphore_signal(barrier, inc=1, device_id=partner, device_id_type=MESH)

    for load in incoming_loads:
        load.wait()
    blocks = incoming_v[...].astype(BF16)
    snd1[...] = blocks.reshape(plane, CORES, admitted * kb, hd)
    pl.semaphore_wait(barrier, len(partners))
    copy0 = remote(snd1.at[:, 1 - c], pair1.at[:, c], s0.at[0], r0.at[0], other)
    copy0.start()
    pair1[:, c] = snd1[:, c]
    copy0.wait_recv()
    for yy, zz in in_plane:
        remote(
            pair1.at[yy * nz + zz],
            rcv1.at[place_yz],
            s1.at[0],
            r1.at[0],
            at(x, yy, zz, c),
        ).start()
    rcv1[place_yz] = pair1[place_yz]
    every1 = all_of(pair1, rcv1, s1.at[0], r1.at[0])

    for load in loads[:7]:
        load.wait()

    q = q_ref[...].astype(F32)
    kk = k_ref[...].astype(F32)
    vv = v_ref[...].astype(F32)
    occupancy = occupancy_ref[...].astype(F32)
    eye = iota((slots, slots), 0) == iota((slots, slots), 1)
    kept = jnp.sum(jnp.where(eye, occupancy, 0.0), axis=1, keepdims=True)
    slot_row = iota((slots, 1), 0)
    taken = jnp.zeros((slots, 1), jnp.bool_)
    lane = iota((1, wide), 1)
    lane_request = (lane // kb) % admitted
    lane_slot = jnp.zeros((1, wide), jnp.int32)
    for a in range(admitted):
        slot = admit_ref[a] - x * slots
        taken = jnp.logical_or(taken, slot_row == slot)
        lane_slot = jnp.where(lane_request == a, slot, lane_slot)
    old_q = jnp.where(taken, 0.0, q * kept)
    lane2 = iota((hd, wide), 1)
    spread_key = (lane2 // (admitted * kb)) * kb + lane2 % kb
    repeat = (iota((hd, wide), 0) == spread_key).astype(BF16)
    new_q = dot(q.astype(BF16), repeat)
    new_q = jnp.where(slot_row == lane_slot, new_q, 0.0).astype(BF16)
    base_old = []
    row8 = iota((8, hd), 0)
    for chunk in range(slots // 8):
        part = old_q[chunk * 8 : chunk * 8 + 8]
        diagonal = jnp.concatenate(
            [jnp.where(row8 == s, part, 0.0) for s in range(8)], axis=1
        ).astype(BF16)
        states = state_v[chunk * 8 * hd : (chunk + 1) * 8 * hd, :].astype(BF16)
        base_old.append(dot(diagonal, states))
    for load in loads[7:9]:
        load.wait()

    position0 = iota((rows, rows), 0)
    position1 = iota((rows, rows), 1)
    row_of0 = natural_row(position0, grid)
    row_of1 = natural_row(position1, grid)
    to_held = (position0 == row_of1).astype(F32)
    not_after = (row_of0 <= row_of1).astype(BF16)
    expert = iota((8, rows), 0) * (nz // 2) + z // 2
    hit = jnp.zeros((8, rows), jnp.bool_)
    weight = jnp.zeros((8, rows), F32)
    for t in range(routes_ref.shape[0]):
        route = jnp.broadcast_to(routes_ref[t : t + 1, :].astype(F32), (8, rows))
        route = dot(route.astype(BF16), to_held.astype(BF16))
        gate_value = jnp.broadcast_to(weight_ref[t : t + 1, :], (8, rows))
        gate_value = dot(gate_value, to_held, precision=lax.Precision.HIGHEST)
        same = route == expert.astype(F32)
        hit = jnp.logical_or(hit, same)
        weight = weight + jnp.where(same, gate_value, 0.0)
    rank = dot(hit.astype(F32).astype(BF16), not_after)
    rank = jnp.where(hit, rank, 0.0)
    place = (iota((CAPACITY, rows), 0) + 1).astype(F32)
    picks, slot_weights = [], []
    for yy in range(ny):
        chosen = rank[yy : yy + 1, :] == place
        picks.append(chosen.astype(F32))
        slot_weights.append(
            jnp.sum(jnp.where(chosen, weight[yy : yy + 1, :], 0.0), axis=1, keepdims=True)
        )
    pick = jnp.concatenate(picks, axis=0).astype(BF16)
    from_held = (position1 == row_of0).astype(BF16)

    every1.wait_recv()
    arrived = rcv1[...].astype(F32).reshape(wide, hd).astype(BF16)
    base = jnp.concatenate(base_old, axis=0) + dot(new_q, arrived)
    raw = jnp.exp(-decay_ref[...]) * base + jnp.sum(q * kk, axis=1, keepdims=True) * vv
    power = jnp.mean(raw * raw, axis=1, keepdims=True)
    heads_buf[x] = (raw * lax.rsqrt(power + EPSILON)).astype(BF16)

    copies2 = []
    for i, xx in enumerate(in_row):
        copy = remote(heads_buf.at[x], heads_buf.at[x], s2.at[i], r2.at[i], at(xx, y, z, c))
        copy.start()
        copies2.append(copy)
    for load in loads[9:12]:
        load.wait()
    for copy in copies2:
        copy.wait_recv()

    heads = heads_buf[...].reshape(rows, hd)
    heads = dot(from_held, heads).astype(BF16)
    row_in_half = iota((half, cols), 0)
    copies3 = []
    for yy in range(ny):
        product = dot(heads, wo_v[:, yy * cols : (yy + 1) * cols])
        partial[yy] = product.reshape(nz, CORES, half, cols)
        res = residual_ref[:, yy * cols : (yy + 1) * cols].astype(F32)
        partial[yy, z, c] += jnp.where(row_in_half == 2 * y, res[0:1, :], 0.0) + jnp.where(
            row_in_half == 2 * y + 1, res[1:2, :], 0.0
        )
        snd3[yy] = partial[yy, :, 1 - c].astype(BF16)
        copy = remote(snd3.at[yy], rcv3.at[yy], s3.at[yy], r3.at[yy], other)
        copy.start()
        copies3.append(copy)

    for yy in range(ny):
        copies3[yy].wait_recv()
        for zz in range(nz):
            snd4[yy * nz + zz] = (partial[yy, zz, c] + rcv3[yy, zz].astype(F32)).astype(BF16)
    for i, (yy, zz) in enumerate(in_plane):
        remote(
            snd4.at[yy * nz + zz], rcv4.at[i], s4.at[0], r4.at[0], at(x, yy, zz, c)
        ).start()
    mine = partial[y, z, c] + rcv3[y, z].astype(F32)
    every4 = all_of(snd4, rcv4, s4.at[0], r4.at[0])
    every4.wait_recv()
    for i in range(plane - 1):
        mine = mine + rcv4[i].astype(F32)
    mixed = mine.astype(BF16)

    full[z, c] = mixed
    copy5 = remote(full.at[z, c], full.at[z, c], s5.at[0], r5.at[0], other)
    copy5.start()
    copy5.wait_recv()
    copies6 = []
    for i, zz in enumerate(in_column):
        copy = remote(full.at[z], full.at[z], s6.at[i], r6.at[i], at(x, y, zz, c))
        copy.start()
        copies6.append(copy)
    for copy in copies6:
        copy.wait_recv()

    every_row = full[...].astype(F32).reshape(rows, cols).astype(BF16)
    picked = dot(pick, every_row).astype(BF16)
    for yy in range(ny):
        snd7[yy] = picked[yy * CAPACITY : (yy + 1) * CAPACITY]
    copies7 = []
    for i, (dx, dy) in enumerate(steps_xy):
        xx, yy = step(x, dx, nx), step(y, dy, ny)
        copy = remote(snd7.at[yy], xin.at[here], s7.at[i], r7.at[i], at(xx, yy, z, c))
        copy.start()
        copies7.append(copy)
    xin[here] = snd7[y]
    for load in loads[12:]:
        load.wait()

    def one_block(block, carry):
        gate_sum, up_sum, squares = carry
        taken_rows = xin[block].astype(F32)
        columns = pl.ds(pl.multiple_of(block * cols, cols), cols)
        squares = squares + jnp.sum(taken_rows * taken_rows, axis=1, keepdims=True)
        scaled = (taken_rows * gain_ref[:, columns]).astype(BF16)
        gate_sum = gate_sum + dot(scaled, gate_v[:, columns], ((1,), (1,)))
        up_sum = up_sum + dot(scaled, up_v[:, columns], ((1,), (1,)))
        return gate_sum, up_sum, squares

    hidden_units = gate_v.shape[0]
    carry = (
        jnp.zeros((CAPACITY, hidden_units), F32),
        jnp.zeros((CAPACITY, hidden_units), F32),
        jnp.zeros((CAPACITY, 1), F32),
    )
    carry = one_block(here, carry)
    for i in reversed(range(nx * ny - 1)):
        dx, dy = steps_xy[i]
        copies7[i].wait_recv()
        carry = one_block(step(x, nx - dx, nx) * ny + step(y, ny - dy, ny), carry)
    gate_sum, up_sum, squares = carry
    scale = lax.rsqrt(squares / (nx * ny * cols) + EPSILON)
    gate_sum = gate_sum * scale
    up_sum = up_sum * scale
    hidden = (gate_sum / (1.0 + jnp.exp(-gate_sum)) * up_sum).astype(BF16)

    def down_block(block):
        columns = pl.ds(pl.multiple_of(block * cols, cols), cols)
        return dot(hidden, down_v[:, columns]).astype(BF16)

    copies8 = []
    for i, (dx, dy) in enumerate(steps_xy):
        xx, yy = step(x, dx, nx), step(y, dy, ny)
        snd8[i] = down_block(xx * ny + yy)
        copy = remote(snd8.at[i], rcv8.at[here], s8.at[i], r8.at[i], at(xx, yy, z, c))
        copy.start()
        copies8.append(copy)
    rcv8[here] = down_block(here)
    for copy in copies8:
        copy.wait_recv()

    summed = []
    for yy in range(ny):
        term = rcv8[yy].astype(F32)
        for xx in range(1, nx):
            term = term + rcv8[xx * ny + yy].astype(F32)
        summed.append(term * slot_weights[yy])
    summed = jnp.concatenate(summed, axis=0).astype(BF16)
    routed = dot(pick, summed, ((0,), (0,)))
    own9[...] = routed.reshape(nz, CORES, half, cols)

    snd9[...] = own9[:, 1 - c].astype(BF16)
    copy9 = remote(snd9, rcv9, s9.at[0], r9.at[0], other)
    copy9.start()
    own9[z, c] += mixed.astype(F32)
    copy9.wait_recv()
    for zz in range(nz):
        block = own9[zz, c] + rcv9[zz].astype(F32)
        for yy in range(ny):
            snd10[yy * nz + zz] = block[2 * yy : 2 * yy + 2, :]
    for yy, zz in in_plane:
        remote(
            snd10.at[yy * nz + zz],
            rcv10.at[place_yz],
            s10.at[0],
            r10.at[0],
            at(x, yy, zz, c),
        ).start()
    rcv10[place_yz] = snd10[place_yz]
    every10 = all_of(snd10, rcv10, s10.at[0], r10.at[0])
    every10.wait_recv()
    for yy in range(ny):
        total = rcv10[yy * nz]
        for zz in range(1, nz):
            total = total + rcv10[yy * nz + zz]
        out_ref[:, yy * cols : (yy + 1) * cols] = total.astype(BF16)

    for copy in [copy0, every1, every4, copy5, copy9, every10]:
        copy.wait_send()
    for copy in copies2 + copies3 + copies6 + copies7 + copies8:
        copy.wait_send()


def body(
    grid,
    residual_in,
    queries,
    keys_new,
    values_new,
    cached_state,
    incoming_state,
    admit_slot,
    occupancy,
    decay_rate,
    out_proj,
    norm_gain,
    routes,
    route_weight,
    gate_proj,
    up_proj,
    down_proj,
):
    nx, ny, nz = grid
    slots, hd = queries.shape
    rows = nx * slots
    half = 2 * ny
    plane = ny * nz
    cols = residual_in.shape[1] // ny
    blocks = nx * ny
    units = gate_proj.shape[2]
    width = gate_proj.shape[1]
    admitted, parts, kb, _ = incoming_state.shape

    vmem = pl.BlockSpec(memory_space=pltpu.VMEM)
    anywhere = pl.BlockSpec(memory_space=pl.ANY)
    dma = lambda n: pltpu.SemaphoreType.DMA((n,))
    scratch = [
        pltpu.VMEM((parts, admitted * kb, hd), F32),
        pltpu.SMEM(admit_slot.shape, jnp.int32),
        pltpu.VMEM((1, slots), jnp.int32),
        pltpu.VMEM((slots, hd), BF16),
        pltpu.VMEM((slots, hd), BF16),
        pltpu.VMEM((slots, hd), BF16),
        pltpu.VMEM((1, 1), F32),
        pltpu.VMEM((routes.shape[1], rows), jnp.int32),
        pltpu.VMEM((routes.shape[1], rows), F32),
        pltpu.VMEM(residual_in.shape, BF16),
        pltpu.VMEM((1, width), F32),
        pltpu.VMEM((slots * hd, hd), F32),
        pltpu.VMEM(out_proj.shape, BF16),
        pltpu.VMEM((units, width), BF16),
        pltpu.VMEM((units, width), BF16),
        pltpu.VMEM((units, width), BF16),
        pltpu.VMEM((plane, CORES, admitted * kb, hd), BF16),
        pltpu.VMEM((plane, CORES, admitted * kb, hd), BF16),
        pltpu.VMEM((plane, CORES, admitted * kb, hd), BF16),
        pltpu.VMEM((nx, slots, hd), BF16),
        pltpu.VMEM((ny, nz, CORES, half, cols), F32),
        pltpu.VMEM((ny, nz, half, cols), BF16),
        pltpu.VMEM((ny, nz, half, cols), BF16),
        pltpu.VMEM((plane, half, cols), BF16),
        pltpu.VMEM((plane, half, cols), BF16),
        pltpu.VMEM((nz, CORES, half, cols), BF16),
        pltpu.VMEM((ny, CAPACITY, cols), BF16),
        pltpu.VMEM((blocks, CAPACITY, cols), BF16),
        pltpu.VMEM((blocks, CAPACITY, cols), BF16),
        pltpu.VMEM((blocks, CAPACITY, cols), BF16),
        pltpu.VMEM((nz, CORES, half, cols), F32),
        pltpu.VMEM((nz, half, cols), BF16),
        pltpu.VMEM((nz, half, cols), BF16),
        pltpu.VMEM((plane, 2, cols), F32),
        pltpu.VMEM((plane, 2, cols), F32),
        dma(admitted + 15),
    ]
    for n in (1, 1, nx - 1, ny, 1, 1, nz - 1, blocks - 1, blocks - 1, 1, 1):
        scratch += [dma(n), dma(n)]

    def kernel(*refs):
        layer_kernel(grid, refs[:16], *refs[16:])

    return pl.pallas_call(
        kernel,
        out_shape=jax.ShapeDtypeStruct(residual_in.shape, BF16),
        in_specs=[anywhere] * 16,
        out_specs=vmem,
        scratch_shapes=scratch,
        compiler_params=pltpu.CompilerParams(
            collective_id=0, has_side_effects=True, vmem_limit_bytes=VMEM_BYTES
        ),
    )(
        incoming_state,
        admit_slot,
        occupancy.reshape(1, slots),
        queries,
        keys_new,
        values_new,
        decay_rate.reshape(1, 1),
        cached_state.reshape(slots * hd, hd),
        routes.T,
        route_weight.T,
        residual_in,
        out_proj,
        norm_gain.reshape(1, width),
        gate_proj[0].T,
        up_proj[0].T,
        down_proj[0],
    )


def solution(mesh):
    in_specs = (
        P("ep", "sec"),
        P("sec", "ep"),
        P("sec", "ep"),
        P("sec", "ep"),
        P("sec", "ep", None, None),
        P("sec", None, "ep", None),
        P("sec"),
        P("sec"),
        P("ep"),
        P("ep", "sec"),
        P(),
        P(),
        P(),
        P("ep", None, "sec"),
        P("ep", None, "sec"),
        P("ep", "sec", None),
    )
    return jax.shard_map(
        functools.partial(body, GRID),
        mesh=mesh,
        in_specs=in_specs,
        out_specs=P("ep", "sec"),
        check_vma=False,
    )
```

```python
import functools

import jax
import jax.numpy as jnp
from jax import lax
from jax.experimental import pallas as pl
from jax.experimental.pallas import tpu as pltpu
from jax.sharding import PartitionSpec as P

EPSILON = 1e-06
CORES = 2
CAPACITY = 32
VMEM_BYTES = 62 * 2**20
MESH = pl.DeviceIdType.MESH
F32 = jnp.float32
BF16 = jnp.bfloat16
GRID = (4, 4, 8)


def iota(shape, dim):
    return lax.broadcasted_iota(jnp.int32, shape, dim)


def natural_row(position, grid):
    _, ny, nz = grid
    half = 2 * ny
    zi = position // (CORES * half)
    ci = (position // half) % CORES
    yi = (position % half) // 2
    return (yi * nz + zi) * (2 * CORES) + ci * 2 + position % 2


def far_first(*sizes):
    steps = [()]
    for size in sizes:
        steps = [step + (i,) for step in steps for i in range(size)]

    def distance(step):
        return sum(min(i, size - i) for i, size in zip(step, sizes))

    return sorted(steps, key=lambda step: -distance(step))[:-1]


def dot(a, b, dims=((1,), (0,)), precision=None):
    return lax.dot_general(a, b, (dims, ((), ())), preferred_element_type=F32, precision=precision)


def layer_kernel(
    grid,
    operands,
    out_ref,
    incoming_v,
    admit_ref,
    occupancy_ref,
    q_ref,
    k_ref,
    v_ref,
    decay_ref,
    routes_ref,
    weight_ref,
    residual_ref,
    gain_ref,
    state_v,
    wo_v,
    gate_v,
    up_v,
    down_v,
    snd1,
    pair1,
    rcv1,
    heads_buf,
    partial,
    snd4,
    rcv4,
    full,
    snd7,
    xin,
    snd8,
    rcv8,
    own9,
    snd9,
    rcv9,
    snd10,
    rcv10,
    local_sem,
    s0,
    r0,
    s1,
    r1,
    s2,
    r2,
    s3,
    r3,
    s4,
    r4,
    s5,
    r5,
    s6,
    r6,
    s7,
    r7,
    s8,
    r8,
    s9,
    r9,
    s10,
    r10,
):
    nx, ny, nz = grid
    slots, hd = q_ref.shape
    parts = ny * nz * CORES
    kb = hd // parts
    rows = nx * slots
    half = 2 * ny
    plane = ny * nz
    cols = xin.shape[2]
    admitted = admit_ref.shape[0]
    wide = parts * admitted * kb

    x = lax.axis_index("sec")
    ep = lax.axis_index("ep")
    c = lax.rem(ep, CORES)
    z = lax.rem(ep // CORES, nz)
    y = ep // (CORES * nz)

    here = x * ny + y
    place_yz = y * nz + z

    def at(xx, yy, zz, cc):
        return (xx, (yy * nz + zz) * CORES + cc)

    def remote(src, dst, send_sem, recv_sem, device):
        return pltpu.make_async_remote_copy(
            src, dst, send_sem, recv_sem, device_id=device, device_id_type=MESH
        )

    def step(start, by, size):
        return lax.rem(start + by, size)

    other = at(x, y, z, 1 - c)
    in_plane = [(step(y, dy, ny), step(z, dz, nz)) for dy, dz in far_first(ny, nz)]
    in_column = [step(z, dz, nz) for (dz,) in far_first(nz)]
    in_row = [(step(x, dx, nx), step(c, dc, CORES)) for dx, dc in far_first(nx, CORES)]
    steps_xy = far_first(nx, ny)

    def all_of(src, dst, send_sem, recv_sem):
        count = plane - 1
        return remote(
            src.at[pl.ds(0, count)], dst.at[pl.ds(0, count)], send_sem, recv_sem, other
        )

    incoming_hbm, *others = operands
    held = (
        admit_ref,
        occupancy_ref,
        q_ref,
        k_ref,
        v_ref,
        decay_ref,
        state_v,
        routes_ref,
        weight_ref,
        residual_ref,
        wo_v.at[c],
        gain_ref,
        gate_v,
        up_v,
        down_v,
    )
    incoming_loads = [
        pltpu.make_async_copy(
            incoming_hbm.at[a], incoming_v.at[:, kb * a : kb * (a + 1), :], local_sem.at[a]
        )
        for a in range(admitted)
    ]
    loads = [
        pltpu.make_async_copy(src, dst, local_sem.at[admitted + i])
        for i, (src, dst) in enumerate(zip(others, held))
    ]
    for load in incoming_loads + loads:
        load.start()

    barrier = pltpu.get_barrier_semaphore()
    partners = [at(x, yy, zz, c) for yy, zz in in_plane] + [other]
    partners += [
        at(step(x, dx, nx), step(y, dy, ny), z, c) for dx, dy in far_first(nx, ny) if dx
    ]
    partners += [at(xx, y, z, 1 - c) for xx in [step(x, dx, nx) for dx in range(1, nx)]]
    for partner in partners:
        pl.semaphore_signal(barrier, inc=1, device_id=partner, device_id_type=MESH)

    for load in incoming_loads:
        load.wait()
    blocks = incoming_v[...].astype(BF16)
    snd1[...] = blocks.reshape(plane, CORES, admitted * kb, hd)
    pl.semaphore_wait(barrier, len(partners))
    copy0 = remote(snd1.at[:, 1 - c], pair1.at[:, c], s0.at[0], r0.at[0], other)
    copy0.start()
    pair1[:, c] = snd1[:, c]
    wo_hbm = others[10]
    copy_wo = remote(wo_hbm, wo_v.at[c], s3.at[0], r3.at[0], other)
    copy_wo.start()
    copy0.wait_recv()
    for yy, zz in in_plane:
        remote(
            pair1.at[yy * nz + zz],
            rcv1.at[place_yz],
            s1.at[0],
            r1.at[0],
            at(x, yy, zz, c),
        ).start()
    rcv1[place_yz] = pair1[place_yz]
    every1 = all_of(pair1, rcv1, s1.at[0], r1.at[0])

    for load in loads[:7]:
        load.wait()

    q = q_ref[...].astype(F32)
    kk = k_ref[...].astype(F32)
    vv = v_ref[...].astype(F32)
    occupancy = occupancy_ref[...].astype(F32)
    eye = iota((slots, slots), 0) == iota((slots, slots), 1)
    kept = jnp.sum(jnp.where(eye, occupancy, 0.0), axis=1, keepdims=True)
    slot_row = iota((slots, 1), 0)
    taken = jnp.zeros((slots, 1), jnp.bool_)
    lane = iota((1, wide), 1)
    lane_request = (lane // kb) % admitted
    lane_slot = jnp.zeros((1, wide), jnp.int32)
    for a in range(admitted):
        slot = admit_ref[a] - x * slots
        taken = jnp.logical_or(taken, slot_row == slot)
        lane_slot = jnp.where(lane_request == a, slot, lane_slot)
    old_q = jnp.where(taken, 0.0, q * kept)
    lane2 = iota((hd, wide), 1)
    spread_key = (lane2 // (admitted * kb)) * kb + lane2 % kb
    repeat = (iota((hd, wide), 0) == spread_key).astype(BF16)
    new_q = dot(q.astype(BF16), repeat)
    new_q = jnp.where(slot_row == lane_slot, new_q, 0.0).astype(BF16)
    base_old = []
    row8 = iota((8, hd), 0)
    for chunk in range(slots // 8):
        part = old_q[chunk * 8 : chunk * 8 + 8]
        diagonal = jnp.concatenate(
            [jnp.where(row8 == s, part, 0.0) for s in range(8)], axis=1
        ).astype(BF16)
        states = state_v[chunk * 8 * hd : (chunk + 1) * 8 * hd, :].astype(BF16)
        base_old.append(dot(diagonal, states))
    for load in loads[7:9]:
        load.wait()

    position0 = iota((rows, rows), 0)
    position1 = iota((rows, rows), 1)
    row_of0 = natural_row(position0, grid)
    row_of1 = natural_row(position1, grid)
    to_held = (position0 == row_of1).astype(F32)
    not_after = (row_of0 <= row_of1).astype(BF16)
    expert = iota((8, rows), 0) * (nz // 2) + z // 2
    hit = jnp.zeros((8, rows), jnp.bool_)
    weight = jnp.zeros((8, rows), F32)
    for t in range(routes_ref.shape[0]):
        route = jnp.broadcast_to(routes_ref[t : t + 1, :].astype(F32), (8, rows))
        route = dot(route.astype(BF16), to_held.astype(BF16))
        gate_value = jnp.broadcast_to(weight_ref[t : t + 1, :], (8, rows))
        gate_value = dot(gate_value, to_held, precision=lax.Precision.HIGHEST)
        same = route == expert.astype(F32)
        hit = jnp.logical_or(hit, same)
        weight = weight + jnp.where(same, gate_value, 0.0)
    rank = dot(hit.astype(F32).astype(BF16), not_after)
    rank = jnp.where(hit, rank, 0.0)
    place = (iota((CAPACITY, rows), 0) + 1).astype(F32)
    picks, slot_weights = [], []
    for yy in range(ny):
        chosen = rank[yy : yy + 1, :] == place
        picks.append(chosen.astype(F32))
        slot_weights.append(
            jnp.sum(jnp.where(chosen, weight[yy : yy + 1, :], 0.0), axis=1, keepdims=True)
        )
    pick = jnp.concatenate(picks, axis=0).astype(BF16)
    mine0 = iota((rows // CORES, rows), 0)
    mine0 = (mine0 // half) * (CORES * half) + c * half + mine0 % half
    mine0 = natural_row(mine0, grid)
    from_held = (iota((rows // CORES, rows), 1) == mine0).astype(BF16)

    every1.wait_recv()
    arrived = rcv1[...].astype(F32).reshape(wide, hd).astype(BF16)
    base = jnp.concatenate(base_old, axis=0) + dot(new_q, arrived)
    raw = jnp.exp(-decay_ref[...]) * base + jnp.sum(q * kk, axis=1, keepdims=True) * vv
    power = jnp.mean(raw * raw, axis=1, keepdims=True)
    heads_buf[c, x] = (raw * lax.rsqrt(power + EPSILON)).astype(BF16)

    copies2 = []
    for i, (xx, cc) in enumerate(in_row):
        copy = remote(
            heads_buf.at[c, x], heads_buf.at[c, x], s2.at[i], r2.at[i], at(xx, y, z, cc)
        )
        copy.start()
        copies2.append(copy)
    for load in loads[9:12]:
        load.wait()
    copy_wo.wait_recv()
    for copy in copies2:
        copy.wait_recv()

    heads = jnp.concatenate(
        [dot(from_held, heads_buf[cc].reshape(rows, hd)).astype(BF16) for cc in range(CORES)],
        axis=1,
    )
    row_in_half = iota((half, cols), 0)
    for yy in range(ny):
        columns = slice(yy * cols, (yy + 1) * cols)
        weights = wo_v[:, :, columns].reshape(CORES * hd, cols)
        partial[yy] = dot(heads, weights).reshape(nz, half, cols)
        res = residual_ref[:, columns].astype(F32)
        partial[yy, z] += jnp.where(row_in_half == 2 * y, res[0:1, :], 0.0) + jnp.where(
            row_in_half == 2 * y + 1, res[1:2, :], 0.0
        )
        snd4[yy * nz : (yy + 1) * nz] = partial[yy].astype(BF16)

    for i, (yy, zz) in enumerate(in_plane):
        remote(
            snd4.at[yy * nz + zz], rcv4.at[i], s4.at[0], r4.at[0], at(x, yy, zz, c)
        ).start()
    mine = partial[y, z]
    every4 = all_of(snd4, rcv4, s4.at[0], r4.at[0])
    every4.wait_recv()
    for i in range(plane - 1):
        mine = mine + rcv4[i].astype(F32)
    mixed = mine.astype(BF16)

    full[z, c] = mixed
    copy5 = remote(full.at[z, c], full.at[z, c], s5.at[0], r5.at[0], other)
    copy5.start()
    copy5.wait_recv()
    copies6 = []
    for i, zz in enumerate(in_column):
        copy = remote(full.at[z], full.at[z], s6.at[i], r6.at[i], at(x, y, zz, c))
        copy.start()
        copies6.append(copy)
    for copy in copies6:
        copy.wait_recv()

    every_row = full[...].astype(F32).reshape(rows, cols).astype(BF16)
    picked = dot(pick, every_row).astype(BF16)
    for yy in range(ny):
        snd7[yy] = picked[yy * CAPACITY : (yy + 1) * CAPACITY]
    copies7 = []
    for i, (dx, dy) in enumerate(steps_xy):
        xx, yy = step(x, dx, nx), step(y, dy, ny)
        copy = remote(snd7.at[yy], xin.at[here], s7.at[i], r7.at[i], at(xx, yy, z, c))
        copy.start()
        copies7.append(copy)
    xin[here] = snd7[y]
    for load in loads[12:]:
        load.wait()

    def one_block(block, carry):
        gate_sum, up_sum, squares = carry
        taken_rows = xin[block].astype(F32)
        columns = pl.ds(pl.multiple_of(block * cols, cols), cols)
        squares = squares + jnp.sum(taken_rows * taken_rows, axis=1, keepdims=True)
        scaled = (taken_rows * gain_ref[:, columns]).astype(BF16)
        gate_sum = gate_sum + dot(scaled, gate_v[:, columns], ((1,), (1,)))
        up_sum = up_sum + dot(scaled, up_v[:, columns], ((1,), (1,)))
        return gate_sum, up_sum, squares

    hidden_units = gate_v.shape[0]
    carry = (
        jnp.zeros((CAPACITY, hidden_units), F32),
        jnp.zeros((CAPACITY, hidden_units), F32),
        jnp.zeros((CAPACITY, 1), F32),
    )
    carry = one_block(here, carry)
    for i in reversed(range(nx * ny - 1)):
        dx, dy = steps_xy[i]
        copies7[i].wait_recv()
        carry = one_block(step(x, nx - dx, nx) * ny + step(y, ny - dy, ny), carry)
    gate_sum, up_sum, squares = carry
    scale = lax.rsqrt(squares / (nx * ny * cols) + EPSILON)
    gate_sum = gate_sum * scale
    up_sum = up_sum * scale
    hidden = (gate_sum / (1.0 + jnp.exp(-gate_sum)) * up_sum).astype(BF16)

    def down_block(block):
        columns = pl.ds(pl.multiple_of(block * cols, cols), cols)
        return dot(hidden, down_v[:, columns]).astype(BF16)

    copies8 = []
    for i, (dx, dy) in enumerate(steps_xy):
        xx, yy = step(x, dx, nx), step(y, dy, ny)
        snd8[i] = down_block(xx * ny + yy)
        copy = remote(snd8.at[i], rcv8.at[here], s8.at[i], r8.at[i], at(xx, yy, z, c))
        copy.start()
        copies8.append(copy)
    rcv8[here] = down_block(here)
    for copy in copies8:
        copy.wait_recv()

    summed = []
    for yy in range(ny):
        term = rcv8[yy].astype(F32)
        for xx in range(1, nx):
            term = term + rcv8[xx * ny + yy].astype(F32)
        summed.append(term * slot_weights[yy])
    summed = jnp.concatenate(summed, axis=0).astype(BF16)
    routed = dot(pick, summed, ((0,), (0,)))
    own9[...] = routed.reshape(nz, CORES, half, cols)

    snd9[...] = own9[:, 1 - c].astype(BF16)
    copy9 = remote(snd9, rcv9, s9.at[0], r9.at[0], other)
    copy9.start()
    own9[z, c] += mixed.astype(F32)
    copy9.wait_recv()
    for zz in range(nz):
        block = own9[zz, c] + rcv9[zz].astype(F32)
        for yy in range(ny):
            snd10[yy * nz + zz] = block[2 * yy : 2 * yy + 2, :]
    for yy, zz in in_plane:
        remote(
            snd10.at[yy * nz + zz],
            rcv10.at[place_yz],
            s10.at[0],
            r10.at[0],
            at(x, yy, zz, c),
        ).start()
    rcv10[place_yz] = snd10[place_yz]
    every10 = all_of(snd10, rcv10, s10.at[0], r10.at[0])
    every10.wait_recv()
    for yy in range(ny):
        total = rcv10[yy * nz]
        for zz in range(1, nz):
            total = total + rcv10[yy * nz + zz]
        out_ref[:, yy * cols : (yy + 1) * cols] = total.astype(BF16)

    for copy in [copy0, copy_wo, every1, every4, copy5, copy9, every10]:
        copy.wait_send()
    for copy in copies2 + copies6 + copies7 + copies8:
        copy.wait_send()


def body(
    grid,
    residual_in,
    queries,
    keys_new,
    values_new,
    cached_state,
    incoming_state,
    admit_slot,
    occupancy,
    decay_rate,
    out_proj,
    norm_gain,
    routes,
    route_weight,
    gate_proj,
    up_proj,
    down_proj,
):
    nx, ny, nz = grid
    slots, hd = queries.shape
    rows = nx * slots
    half = 2 * ny
    plane = ny * nz
    cols = residual_in.shape[1] // ny
    blocks = nx * ny
    units = gate_proj.shape[2]
    width = gate_proj.shape[1]
    admitted, parts, kb, _ = incoming_state.shape

    vmem = pl.BlockSpec(memory_space=pltpu.VMEM)
    anywhere = pl.BlockSpec(memory_space=pl.ANY)
    dma = lambda n: pltpu.SemaphoreType.DMA((n,))
    scratch = [
        pltpu.VMEM((parts, admitted * kb, hd), F32),
        pltpu.SMEM(admit_slot.shape, jnp.int32),
        pltpu.VMEM((1, slots), jnp.int32),
        pltpu.VMEM((slots, hd), BF16),
        pltpu.VMEM((slots, hd), BF16),
        pltpu.VMEM((slots, hd), BF16),
        pltpu.VMEM((1, 1), F32),
        pltpu.VMEM((routes.shape[1], rows), jnp.int32),
        pltpu.VMEM((routes.shape[1], rows), F32),
        pltpu.VMEM(residual_in.shape, BF16),
        pltpu.VMEM((1, width), F32),
        pltpu.VMEM((slots * hd, hd), F32),
        pltpu.VMEM((CORES,) + out_proj.shape, BF16),
        pltpu.VMEM((units, width), BF16),
        pltpu.VMEM((units, width), BF16),
        pltpu.VMEM((units, width), BF16),
        pltpu.VMEM((plane, CORES, admitted * kb, hd), BF16),
        pltpu.VMEM((plane, CORES, admitted * kb, hd), BF16),
        pltpu.VMEM((plane, CORES, admitted * kb, hd), BF16),
        pltpu.VMEM((CORES, nx, slots, hd), BF16),
        pltpu.VMEM((ny, nz, half, cols), F32),
        pltpu.VMEM((plane, half, cols), BF16),
        pltpu.VMEM((plane, half, cols), BF16),
        pltpu.VMEM((nz, CORES, half, cols), BF16),
        pltpu.VMEM((ny, CAPACITY, cols), BF16),
        pltpu.VMEM((blocks, CAPACITY, cols), BF16),
        pltpu.VMEM((blocks, CAPACITY, cols), BF16),
        pltpu.VMEM((blocks, CAPACITY, cols), BF16),
        pltpu.VMEM((nz, CORES, half, cols), F32),
        pltpu.VMEM((nz, half, cols), BF16),
        pltpu.VMEM((nz, half, cols), BF16),
        pltpu.VMEM((plane, 2, cols), F32),
        pltpu.VMEM((plane, 2, cols), F32),
        dma(admitted + 15),
    ]
    for n in (1, 1, nx * CORES - 1, 1, 1, 1, nz - 1, blocks - 1, blocks - 1, 1, 1):
        scratch += [dma(n), dma(n)]

    def kernel(*refs):
        layer_kernel(grid, refs[:16], *refs[16:])

    return pl.pallas_call(
        kernel,
        out_shape=pltpu.VMEM(residual_in.shape, BF16),
        in_specs=[anywhere] * 16,
        out_specs=vmem,
        scratch_shapes=scratch,
        compiler_params=pltpu.CompilerParams(
            collective_id=0, has_side_effects=True, vmem_limit_bytes=VMEM_BYTES
        ),
    )(
        incoming_state,
        admit_slot,
        occupancy.reshape(1, slots),
        queries,
        keys_new,
        values_new,
        decay_rate.reshape(1, 1),
        cached_state.reshape(slots * hd, hd),
        routes.T,
        route_weight.T,
        residual_in,
        out_proj,
        norm_gain.reshape(1, width),
        gate_proj[0].T,
        up_proj[0].T,
        down_proj[0],
    )


def solution(mesh):
    in_specs = (
        P("ep", "sec"),
        P("sec", "ep"),
        P("sec", "ep"),
        P("sec", "ep"),
        P("sec", "ep", None, None),
        P("sec", None, "ep", None),
        P("sec"),
        P("sec"),
        P("ep"),
        P("ep", "sec"),
        P(),
        P(),
        P(),
        P("ep", None, "sec"),
        P("ep", None, "sec"),
        P("ep", "sec", None),
    )
    return jax.shard_map(
        functools.partial(body, GRID),
        mesh=mesh,
        in_specs=in_specs,
        out_specs=P("ep", "sec"),
        check_vma=False,
    )
```

```python
import functools

import jax
import jax.numpy as jnp
from jax import lax
from jax.experimental import pallas as pl
from jax.experimental.pallas import tpu as pltpu
from jax.sharding import PartitionSpec as P

EPSILON = 1e-06
CORES = 2
CAPACITY = 32
VMEM_BYTES = 62 * 2**20
MESH = pl.DeviceIdType.MESH
F32 = jnp.float32
BF16 = jnp.bfloat16
GRID = (4, 4, 8)


def iota(shape, dim):
    return lax.broadcasted_iota(jnp.int32, shape, dim)


def natural_row(position, grid):
    _, ny, nz = grid
    half = 2 * ny
    zi = position // (CORES * half)
    ci = (position // half) % CORES
    yi = (position % half) // 2
    return (yi * nz + zi) * (2 * CORES) + ci * 2 + position % 2


def far_first(*sizes):
    steps = [()]
    for size in sizes:
        steps = [step + (i,) for step in steps for i in range(size)]

    def distance(step):
        return sum(min(i, size - i) for i, size in zip(step, sizes))

    return sorted(steps, key=lambda step: -distance(step))[:-1]


def dot(a, b, dims=((1,), (0,)), precision=None):
    return lax.dot_general(a, b, (dims, ((), ())), preferred_element_type=F32, precision=precision)


def layer_kernel(
    grid,
    operands,
    out_ref,
    incoming_v,
    admit_ref,
    occupancy_ref,
    q_ref,
    k_ref,
    v_ref,
    decay_ref,
    routes_ref,
    weight_ref,
    residual_ref,
    gain_ref,
    state_v,
    wo_v,
    gate_v,
    up_v,
    down_v,
    snd1,
    pair1,
    rcv1,
    heads_buf,
    residual_buf,
    summed8,
    snd4,
    rcv4,
    full,
    snd7,
    xin,
    snd8,
    rcv8,
    own9,
    snd9,
    rcv9,
    snd10,
    rcv10,
    local_sem,
    s_res,
    r_res,
    s0,
    r0,
    s1,
    r1,
    s2,
    r2,
    s3,
    r3,
    s4,
    r4,
    s5,
    r5,
    s6,
    r6,
    s7,
    r7,
    s8,
    r8,
    s9,
    r9,
    s10,
    r10,
):
    nx, ny, nz = grid
    slots, hd = q_ref.shape
    parts = ny * nz * CORES
    kb = hd // parts
    rows = nx * slots
    half = 2 * ny
    plane = ny * nz
    cols = xin.shape[2]
    admitted = admit_ref.shape[0]
    wide = parts * admitted * kb

    x = lax.axis_index("sec")
    ep = lax.axis_index("ep")
    c = lax.rem(ep, CORES)
    z = lax.rem(ep // CORES, nz)
    y = ep // (CORES * nz)

    here = x * ny + y
    place_yz = y * nz + z

    def at(xx, yy, zz, cc):
        return (xx, (yy * nz + zz) * CORES + cc)

    def remote(src, dst, send_sem, recv_sem, device):
        return pltpu.make_async_remote_copy(
            src, dst, send_sem, recv_sem, device_id=device, device_id_type=MESH
        )

    def step(start, by, size):
        return lax.rem(start + by, size)

    other = at(x, y, z, 1 - c)
    in_plane = [(step(y, dy, ny), step(z, dz, nz)) for dy, dz in far_first(ny, nz)]
    in_column = [step(z, dz, nz) for (dz,) in far_first(nz)]
    in_row = [(step(x, dx, nx), step(c, dc, CORES)) for dx, dc in far_first(nx, CORES)]
    steps_xy = far_first(nx, ny)

    def all_of(src, dst, send_sem, recv_sem):
        count = plane - 1
        return remote(
            src.at[pl.ds(0, count)], dst.at[pl.ds(0, count)], send_sem, recv_sem, other
        )

    incoming_hbm, *others = operands
    held = (
        admit_ref,
        occupancy_ref,
        q_ref,
        k_ref,
        v_ref,
        decay_ref,
        state_v,
        routes_ref,
        weight_ref,
        residual_ref,
        wo_v.at[c],
        gain_ref,
        gate_v,
        up_v,
        down_v,
    )
    incoming_loads = [
        pltpu.make_async_copy(
            incoming_hbm.at[a], incoming_v.at[:, kb * a : kb * (a + 1), :], local_sem.at[a]
        )
        for a in range(admitted)
    ]
    loads = [
        pltpu.make_async_copy(src, dst, local_sem.at[admitted + i])
        for i, (src, dst) in enumerate(zip(others, held))
    ]
    for load in incoming_loads:
        load.start()

    barrier = pltpu.get_barrier_semaphore()
    partners = [at(x, yy, zz, c) for yy, zz in in_plane] + [other]
    partners += [
        at(step(x, dx, nx), step(y, dy, ny), z, c) for dx, dy in far_first(nx, ny) if dx
    ]
    partners += [at(xx, y, z, 1 - c) for xx in [step(x, dx, nx) for dx in range(1, nx)]]
    for partner in partners:
        pl.semaphore_signal(barrier, inc=1, device_id=partner, device_id_type=MESH)
    for load in loads:
        load.start()

    for load in incoming_loads:
        load.wait()
    blocks = incoming_v[...].astype(BF16)
    snd1[...] = blocks.reshape(plane, CORES, admitted * kb, hd)
    pl.semaphore_wait(barrier, len(partners))
    copy0 = remote(snd1.at[:, 1 - c], pair1.at[:, c], s0.at[0], r0.at[0], other)
    copy0.start()
    pair1[:, c] = snd1[:, c]
    wo_hbm = others[10]
    copy_wo = remote(wo_hbm, wo_v.at[c], s3.at[0], r3.at[0], other)
    copy_wo.start()
    copy0.wait_recv()
    for yy, zz in in_plane:
        remote(
            pair1.at[yy * nz + zz],
            rcv1.at[place_yz],
            s1.at[0],
            r1.at[0],
            at(x, yy, zz, c),
        ).start()
    rcv1[place_yz] = pair1[place_yz]
    every1 = all_of(pair1, rcv1, s1.at[0], r1.at[0])

    loads[9].wait()
    copies_res = []
    for i, (dy,) in enumerate(far_first(ny)):
        yy = step(y, dy, ny)
        columns = pl.ds(pl.multiple_of(yy * cols, cols), cols)
        copy = remote(
            residual_ref.at[:, columns],
            residual_buf.at[y],
            s_res.at[i],
            r_res.at[i],
            at(x, yy, z, c),
        )
        copy.start()
        copies_res.append(copy)
    residual_buf[y] = residual_ref[:, pl.ds(pl.multiple_of(y * cols, cols), cols)]

    for load in loads[:7]:
        load.wait()

    q = q_ref[...].astype(F32)
    kk = k_ref[...].astype(F32)
    vv = v_ref[...].astype(F32)
    occupancy = occupancy_ref[...].astype(F32)
    eye = iota((slots, slots), 0) == iota((slots, slots), 1)
    kept = jnp.sum(jnp.where(eye, occupancy, 0.0), axis=1, keepdims=True)
    slot_row = iota((slots, 1), 0)
    taken = jnp.zeros((slots, 1), jnp.bool_)
    lane = iota((1, wide), 1)
    lane_request = (lane // kb) % admitted
    lane_slot = jnp.zeros((1, wide), jnp.int32)
    for a in range(admitted):
        slot = admit_ref[a] - x * slots
        taken = jnp.logical_or(taken, slot_row == slot)
        lane_slot = jnp.where(lane_request == a, slot, lane_slot)
    old_q = jnp.where(taken, 0.0, q * kept)
    lane2 = iota((hd, wide), 1)
    spread_key = (lane2 // (admitted * kb)) * kb + lane2 % kb
    repeat = (iota((hd, wide), 0) == spread_key).astype(BF16)
    new_q = dot(q.astype(BF16), repeat)
    new_q = jnp.where(slot_row == lane_slot, new_q, 0.0).astype(BF16)
    base_old = []
    row8 = iota((8, hd), 0)
    for chunk in range(slots // 8):
        part = old_q[chunk * 8 : chunk * 8 + 8]
        diagonal = jnp.concatenate(
            [jnp.where(row8 == s, part, 0.0) for s in range(8)], axis=1
        ).astype(BF16)
        states = state_v[chunk * 8 * hd : (chunk + 1) * 8 * hd, :].astype(BF16)
        base_old.append(dot(diagonal, states))
    decay = jnp.exp(-decay_ref[...])
    old_part = decay * jnp.concatenate(base_old, axis=0)
    old_part = old_part + jnp.sum(q * kk, axis=1, keepdims=True) * vv

    for load in loads[7:9]:
        load.wait()

    position0 = iota((rows, rows), 0)
    position1 = iota((rows, rows), 1)
    row_of0 = natural_row(position0, grid)
    row_of1 = natural_row(position1, grid)
    to_held = (position0 == row_of1).astype(F32)
    not_after = (row_of0 <= row_of1).astype(BF16)
    expert = iota((8, rows), 0) * (nz // 2) + z // 2
    hit = jnp.zeros((8, rows), jnp.bool_)
    weight = jnp.zeros((8, rows), F32)
    for t in range(routes_ref.shape[0]):
        route = jnp.broadcast_to(routes_ref[t : t + 1, :].astype(F32), (8, rows))
        route = dot(route.astype(BF16), to_held.astype(BF16))
        gate_value = jnp.broadcast_to(weight_ref[t : t + 1, :], (8, rows))
        gate_value = dot(gate_value, to_held, precision=lax.Precision.HIGHEST)
        same = route == expert.astype(F32)
        hit = jnp.logical_or(hit, same)
        weight = weight + jnp.where(same, gate_value, 0.0)
    rank = dot(hit.astype(F32).astype(BF16), not_after)
    rank = jnp.where(hit, rank, 0.0)
    place = (iota((CAPACITY, rows), 0) + 1).astype(F32)
    picks, slot_weights = [], []
    for yy in range(ny):
        chosen = rank[yy : yy + 1, :] == place
        picks.append(chosen.astype(F32))
        slot_weights.append(
            jnp.sum(jnp.where(chosen, weight[yy : yy + 1, :], 0.0), axis=1, keepdims=True)
        )
    pick = jnp.concatenate(picks, axis=0)
    place_rows = pick.T.astype(BF16)
    pick = pick.astype(BF16)
    mine0 = iota((rows // CORES, rows), 0)
    mine0 = (mine0 // half) * (CORES * half) + c * half + mine0 % half
    mine0 = natural_row(mine0, grid)
    from_held = (iota((rows // CORES, rows), 1) == mine0).astype(BF16)

    every1.wait_recv()
    arrived = rcv1[...].astype(F32).reshape(wide, hd).astype(BF16)
    raw = old_part + decay * dot(new_q, arrived)
    power = jnp.mean(raw * raw, axis=1, keepdims=True)
    heads_buf[c, x] = (raw * lax.rsqrt(power + EPSILON)).astype(BF16)

    copies2 = []
    for i, (xx, cc) in enumerate(in_row):
        copy = remote(
            heads_buf.at[c, x], heads_buf.at[c, x], s2.at[i], r2.at[i], at(xx, y, z, cc)
        )
        copy.start()
        copies2.append(copy)
    for load in loads[10:12]:
        load.wait()
    copy_wo.wait_recv()
    for copy in copies2:
        copy.wait_recv()

    heads = jnp.concatenate(
        [dot(from_held, heads_buf[cc].reshape(rows, hd)).astype(BF16) for cc in range(CORES)],
        axis=1,
    )
    for yy in range(ny):
        weights = wo_v[:, :, yy * cols : (yy + 1) * cols].reshape(CORES * hd, cols)
        product = dot(heads, weights).astype(BF16)
        snd4[yy * nz : (yy + 1) * nz] = product.reshape(nz, half, cols)

    for i, (yy, zz) in enumerate(in_plane):
        remote(
            snd4.at[yy * nz + zz], rcv4.at[i], s4.at[0], r4.at[0], at(x, yy, zz, c)
        ).start()
    every4 = all_of(snd4, rcv4, s4.at[0], r4.at[0])
    for copy in copies_res:
        copy.wait_recv()
    mine = snd4[place_yz].astype(F32) + jnp.concatenate(
        [residual_buf[yy].astype(F32) for yy in range(ny)], axis=0
    )
    for copy in [copy0, copy_wo, every1] + copies2 + copies_res:
        copy.wait_send()
    every4.wait_recv()
    for i in range(plane - 1):
        mine = mine + rcv4[i].astype(F32)
    mixed = mine.astype(BF16)

    full[z, c] = mixed
    copy5 = remote(full.at[z, c], full.at[z, c], s5.at[0], r5.at[0], other)
    copy5.start()
    copy5.wait_recv()
    copies6 = []
    for i, zz in enumerate(in_column):
        copy = remote(full.at[z], full.at[z], s6.at[i], r6.at[i], at(x, y, zz, c))
        copy.start()
        copies6.append(copy)
    for copy in [every4, copy5]:
        copy.wait_send()
    for copy in copies6:
        copy.wait_recv()

    every_row = full[...].astype(F32).reshape(rows, cols).astype(BF16)
    picked = dot(pick, every_row).astype(BF16)
    for yy in range(ny):
        snd7[yy] = picked[yy * CAPACITY : (yy + 1) * CAPACITY]
    copies7 = []
    for i, (dx, dy) in enumerate(steps_xy):
        xx, yy = step(x, dx, nx), step(y, dy, ny)
        copy = remote(snd7.at[yy], xin.at[here], s7.at[i], r7.at[i], at(xx, yy, z, c))
        copy.start()
        copies7.append(copy)
    xin[here] = snd7[y]
    for copy in copies6:
        copy.wait_send()
    for load in loads[12:]:
        load.wait()

    def one_block(block, carry):
        gate_sum, up_sum, squares = carry
        taken_rows = xin[block].astype(F32)
        columns = pl.ds(pl.multiple_of(block * cols, cols), cols)
        squares = squares + jnp.sum(taken_rows * taken_rows, axis=1, keepdims=True)
        scaled = (taken_rows * gain_ref[:, columns]).astype(BF16)
        gate_sum = gate_sum + dot(scaled, gate_v[:, columns], ((1,), (1,)))
        up_sum = up_sum + dot(scaled, up_v[:, columns], ((1,), (1,)))
        return gate_sum, up_sum, squares

    hidden_units = gate_v.shape[0]
    carry = (
        jnp.zeros((CAPACITY, hidden_units), F32),
        jnp.zeros((CAPACITY, hidden_units), F32),
        jnp.zeros((CAPACITY, 1), F32),
    )
    carry = one_block(here, carry)
    for i in reversed(range(nx * ny - 1)):
        dx, dy = steps_xy[i]
        copies7[i].wait_recv()
        carry = one_block(step(x, nx - dx, nx) * ny + step(y, ny - dy, ny), carry)
    gate_sum, up_sum, squares = carry
    scale = lax.rsqrt(squares / (nx * ny * cols) + EPSILON)
    gate_sum = gate_sum * scale
    up_sum = up_sum * scale
    hidden = (gate_sum / (1.0 + jnp.exp(-gate_sum)) * up_sum).astype(BF16)

    def down_block(block):
        columns = pl.ds(pl.multiple_of(block * cols, cols), cols)
        return dot(hidden, down_v[:, columns]).astype(BF16)

    copies8 = []
    for i, (dx, dy) in enumerate(steps_xy):
        xx, yy = step(x, dx, nx), step(y, dy, ny)
        snd8[i] = down_block(xx * ny + yy)
        copy = remote(snd8.at[i], rcv8.at[here], s8.at[i], r8.at[i], at(xx, yy, z, c))
        copy.start()
        copies8.append(copy)
    block = dot(hidden, down_v[:, pl.ds(pl.multiple_of(here * cols, cols), cols)])
    for yy in range(1, ny):
        summed8[step(y, yy, ny)] = jnp.zeros(block.shape, F32)
    summed8[y] = block
    for copy in copies7:
        copy.wait_send()
    for i in reversed(range(nx * ny - 1)):
        dx, dy = steps_xy[i]
        xx, yy = step(x, nx - dx, nx), step(y, ny - dy, ny)
        copies8[i].wait_recv()
        summed8[yy] += rcv8[xx * ny + yy].astype(F32)

    summed = [summed8[yy] * slot_weights[yy] for yy in range(ny)]
    summed = jnp.concatenate(summed, axis=0).astype(BF16)
    routed = dot(place_rows, summed)
    own9[...] = routed.reshape(nz, CORES, half, cols)

    snd9[...] = own9[:, 1 - c].astype(BF16)
    copy9 = remote(snd9, rcv9, s9.at[0], r9.at[0], other)
    copy9.start()
    own9[z, c] += mixed.astype(F32)
    copy9.wait_recv()
    for zz in range(nz):
        block = own9[zz, c] + rcv9[zz].astype(F32)
        for yy in range(ny):
            snd10[yy * nz + zz] = block[2 * yy : 2 * yy + 2, :]
    for yy, zz in in_plane:
        remote(
            snd10.at[yy * nz + zz],
            rcv10.at[place_yz],
            s10.at[0],
            r10.at[0],
            at(x, yy, zz, c),
        ).start()
    rcv10[place_yz] = snd10[place_yz]
    every10 = all_of(snd10, rcv10, s10.at[0], r10.at[0])
    for copy in copies8 + [copy9]:
        copy.wait_send()
    every10.wait_recv()
    for yy in range(ny):
        total = rcv10[yy * nz]
        for zz in range(1, nz):
            total = total + rcv10[yy * nz + zz]
        out_ref[:, yy * cols : (yy + 1) * cols] = total.astype(BF16)

    every10.wait_send()


def body(
    grid,
    residual_in,
    queries,
    keys_new,
    values_new,
    cached_state,
    incoming_state,
    admit_slot,
    occupancy,
    decay_rate,
    out_proj,
    norm_gain,
    routes,
    route_weight,
    gate_proj,
    up_proj,
    down_proj,
):
    nx, ny, nz = grid
    slots, hd = queries.shape
    rows = nx * slots
    half = 2 * ny
    plane = ny * nz
    cols = residual_in.shape[1] // ny
    blocks = nx * ny
    units = gate_proj.shape[2]
    width = gate_proj.shape[1]
    admitted, parts, kb, _ = incoming_state.shape

    vmem = pl.BlockSpec(memory_space=pltpu.VMEM)
    anywhere = pl.BlockSpec(memory_space=pl.ANY)
    dma = lambda n: pltpu.SemaphoreType.DMA((n,))
    scratch = [
        pltpu.VMEM((parts, admitted * kb, hd), F32),
        pltpu.SMEM(admit_slot.shape, jnp.int32),
        pltpu.VMEM((1, slots), jnp.int32),
        pltpu.VMEM((slots, hd), BF16),
        pltpu.VMEM((slots, hd), BF16),
        pltpu.VMEM((slots, hd), BF16),
        pltpu.VMEM((1, 1), F32),
        pltpu.VMEM((routes.shape[1], rows), jnp.int32),
        pltpu.VMEM((routes.shape[1], rows), F32),
        pltpu.VMEM(residual_in.shape, BF16),
        pltpu.VMEM((1, width), F32),
        pltpu.VMEM((slots * hd, hd), F32),
        pltpu.VMEM((CORES,) + out_proj.shape, BF16),
        pltpu.VMEM((units, width), BF16),
        pltpu.VMEM((units, width), BF16),
        pltpu.VMEM((units, width), BF16),
        pltpu.VMEM((plane, CORES, admitted * kb, hd), BF16),
        pltpu.VMEM((plane, CORES, admitted * kb, hd), BF16),
        pltpu.VMEM((plane, CORES, admitted * kb, hd), BF16),
        pltpu.VMEM((CORES, nx, slots, hd), BF16),
        pltpu.VMEM((ny, 2, cols), BF16),
        pltpu.VMEM((ny, CAPACITY, cols), F32),
        pltpu.VMEM((plane, half, cols), BF16),
        pltpu.VMEM((plane, half, cols), BF16),
        pltpu.VMEM((nz, CORES, half, cols), BF16),
        pltpu.VMEM((ny, CAPACITY, cols), BF16),
        pltpu.VMEM((blocks, CAPACITY, cols), BF16),
        pltpu.VMEM((blocks, CAPACITY, cols), BF16),
        pltpu.VMEM((blocks, CAPACITY, cols), BF16),
        pltpu.VMEM((nz, CORES, half, cols), F32),
        pltpu.VMEM((nz, half, cols), BF16),
        pltpu.VMEM((nz, half, cols), BF16),
        pltpu.VMEM((plane, 2, cols), F32),
        pltpu.VMEM((plane, 2, cols), F32),
        dma(admitted + 15),
    ]
    for n in (ny - 1, 1, 1, nx * CORES - 1, 1, 1, 1, nz - 1, blocks - 1, blocks - 1, 1, 1):
        scratch += [dma(n), dma(n)]

    def kernel(*refs):
        layer_kernel(grid, refs[:16], *refs[16:])

    return pl.pallas_call(
        kernel,
        out_shape=pltpu.VMEM(residual_in.shape, BF16),
        in_specs=[anywhere] * 16,
        out_specs=vmem,
        scratch_shapes=scratch,
        compiler_params=pltpu.CompilerParams(
            collective_id=0, has_side_effects=True, vmem_limit_bytes=VMEM_BYTES
        ),
    )(
        incoming_state,
        admit_slot,
        occupancy.reshape(1, slots),
        queries,
        keys_new,
        values_new,
        decay_rate.reshape(1, 1),
        cached_state.reshape(slots * hd, hd),
        routes.T,
        route_weight.T,
        residual_in,
        out_proj,
        norm_gain.reshape(1, width),
        gate_proj[0].T,
        up_proj[0].T,
        down_proj[0],
    )


def solution(mesh):
    in_specs = (
        P("ep", "sec"),
        P("sec", "ep"),
        P("sec", "ep"),
        P("sec", "ep"),
        P("sec", "ep", None, None),
        P("sec", None, "ep", None),
        P("sec"),
        P("sec"),
        P("ep"),
        P("ep", "sec"),
        P(),
        P(),
        P(),
        P("ep", None, "sec"),
        P("ep", None, "sec"),
        P("ep", "sec", None),
    )
    return jax.shard_map(
        functools.partial(body, GRID),
        mesh=mesh,
        in_specs=in_specs,
        out_specs=P("ep", "sec"),
        check_vma=False,
    )
```

```python
import functools

import jax
import jax.numpy as jnp
from jax import lax
from jax.experimental import pallas as pl
from jax.experimental.pallas import tpu as pltpu
from jax.sharding import PartitionSpec as P

EPSILON = 1e-06
CORES = 2
CAPACITY = 32
VMEM_BYTES = 62 * 2**20
MESH = pl.DeviceIdType.MESH
F32 = jnp.float32
BF16 = jnp.bfloat16
GRID = (4, 4, 8)


def iota(shape, dim):
    return lax.broadcasted_iota(jnp.int32, shape, dim)


def natural_row(position, grid):
    _, ny, nz = grid
    half = 2 * ny
    zi = position // (CORES * half)
    ci = (position // half) % CORES
    yi = (position % half) // 2
    return (yi * nz + zi) * (2 * CORES) + ci * 2 + position % 2


def far_first(*sizes):
    steps = [()]
    for size in sizes:
        steps = [step + (i,) for step in steps for i in range(size)]

    def distance(step):
        return sum(min(i, size - i) for i, size in zip(step, sizes))

    return sorted(steps, key=lambda step: -distance(step))[:-1]


def dot(a, b, dims=((1,), (0,)), precision=None):
    return lax.dot_general(a, b, (dims, ((), ())), preferred_element_type=F32, precision=precision)


def layer_kernel(
    grid,
    operands,
    out_ref,
    incoming_v,
    admit_ref,
    occupancy_ref,
    q_ref,
    k_ref,
    v_ref,
    decay_ref,
    routes_ref,
    weight_ref,
    residual_ref,
    gain_ref,
    state_v,
    wo_v,
    gate_v,
    up_v,
    down_v,
    snd1,
    rcv1,
    heads_buf,
    partial,
    snd4,
    rcv4,
    full,
    snd7,
    xin,
    snd8,
    rcv8,
    own9,
    snd9,
    rcv9,
    snd10,
    rcv10,
    local_sem,
    s1,
    r1,
    s2,
    r2,
    s3,
    r3,
    s4,
    r4,
    s6,
    r6,
    s7,
    r7,
    s8,
    r8,
    s9,
    r9,
    s10,
    r10,
):
    nx, ny, nz = grid
    slots, hd = q_ref.shape
    parts = ny * nz * CORES
    kb = hd // parts
    rows = nx * slots
    half = 2 * ny
    plane = ny * nz
    cols = xin.shape[2]
    admitted = admit_ref.shape[0]
    wide = parts * admitted * kb

    x = lax.axis_index("sec")
    ep = lax.axis_index("ep")
    c = lax.rem(ep, CORES)
    z = lax.rem(ep // CORES, nz)
    y = ep // (CORES * nz)

    here = x * ny + y
    place_yz = y * nz + z

    def at(xx, yy, zz, cc):
        return (xx, (yy * nz + zz) * CORES + cc)

    def remote(src, dst, send_sem, recv_sem, device):
        return pltpu.make_async_remote_copy(
            src, dst, send_sem, recv_sem, device_id=device, device_id_type=MESH
        )

    def step(start, by, size):
        return lax.rem(start + by, size)

    other = at(x, y, z, 1 - c)
    in_ep = [
        (step(y, dy, ny), step(z, dz, nz), step(c, dc, CORES))
        for dy, dz, dc in far_first(ny, nz, CORES)
    ]
    in_plane = [(step(y, dy, ny), step(z, dz, nz)) for dy, dz in far_first(ny, nz)]
    in_column = [(step(z, dz, nz), step(c, dc, CORES)) for dz, dc in far_first(nz, CORES)]
    in_row = [(step(x, dx, nx), step(c, dc, CORES)) for dx, dc in far_first(nx, CORES)]
    steps_xy = far_first(nx, ny)

    def all_of(src, dst, send_sem, recv_sem):
        count = plane - 1
        return remote(
            src.at[pl.ds(0, count)], dst.at[pl.ds(0, count)], send_sem, recv_sem, other
        )

    incoming_hbm, *others = operands
    held = (
        admit_ref,
        occupancy_ref,
        q_ref,
        k_ref,
        v_ref,
        decay_ref,
        state_v,
        routes_ref,
        weight_ref,
        residual_ref,
        wo_v.at[c],
        gain_ref,
        gate_v,
        up_v,
        down_v,
    )
    incoming_loads = [
        pltpu.make_async_copy(
            incoming_hbm.at[a], incoming_v.at[:, kb * a : kb * (a + 1), :], local_sem.at[a]
        )
        for a in range(admitted)
    ]
    loads = [
        pltpu.make_async_copy(src, dst, local_sem.at[admitted + i])
        for i, (src, dst) in enumerate(zip(others, held))
    ]
    for load in incoming_loads + loads:
        load.start()

    barrier = pltpu.get_barrier_semaphore()
    partners = [at(x, yy, zz, cc) for yy, zz, cc in in_ep]
    partners += [
        at(step(x, dx, nx), step(y, dy, ny), z, c) for dx, dy in far_first(nx, ny) if dx
    ]
    partners += [at(xx, y, z, 1 - c) for xx in [step(x, dx, nx) for dx in range(1, nx)]]
    for partner in partners:
        pl.semaphore_signal(barrier, inc=1, device_id=partner, device_id_type=MESH)

    for load in incoming_loads:
        load.wait()
    snd1[...] = incoming_v[...].astype(BF16)
    pl.semaphore_wait(barrier, len(partners))
    wo_hbm = others[10]
    copy_wo = remote(wo_hbm, wo_v.at[c], s3.at[0], r3.at[0], other)
    for yy, zz, cc in in_ep:
        remote(
            snd1.at[(yy * nz + zz) * CORES + cc],
            rcv1.at[ep],
            s1.at[0],
            r1.at[0],
            at(x, yy, zz, cc),
        ).start()
    rcv1[ep] = snd1[ep]
    copy_wo.start()
    every1 = remote(
        snd1.at[pl.ds(0, parts - 1)],
        rcv1.at[pl.ds(0, parts - 1)],
        s1.at[0],
        r1.at[0],
        other,
    )

    for load in loads[:7]:
        load.wait()

    q = q_ref[...].astype(F32)
    kk = k_ref[...].astype(F32)
    vv = v_ref[...].astype(F32)
    occupancy = occupancy_ref[...].astype(F32)
    eye = iota((slots, slots), 0) == iota((slots, slots), 1)
    kept = jnp.sum(jnp.where(eye, occupancy, 0.0), axis=1, keepdims=True)
    slot_row = iota((slots, 1), 0)
    taken = jnp.zeros((slots, 1), jnp.bool_)
    lane = iota((1, wide), 1)
    lane_request = (lane // kb) % admitted
    lane_slot = jnp.zeros((1, wide), jnp.int32)
    for a in range(admitted):
        slot = admit_ref[a] - x * slots
        taken = jnp.logical_or(taken, slot_row == slot)
        lane_slot = jnp.where(lane_request == a, slot, lane_slot)
    old_q = jnp.where(taken, 0.0, q * kept)
    lane2 = iota((hd, wide), 1)
    spread_key = (lane2 // (admitted * kb)) * kb + lane2 % kb
    repeat = (iota((hd, wide), 0) == spread_key).astype(BF16)
    new_q = dot(q.astype(BF16), repeat)
    new_q = jnp.where(slot_row == lane_slot, new_q, 0.0).astype(BF16)
    base_old = []
    row8 = iota((8, hd), 0)
    for chunk in range(slots // 8):
        part = old_q[chunk * 8 : chunk * 8 + 8]
        diagonal = jnp.concatenate(
            [jnp.where(row8 == s, part, 0.0) for s in range(8)], axis=1
        ).astype(BF16)
        states = state_v[chunk * 8 * hd : (chunk + 1) * 8 * hd, :].astype(BF16)
        base_old.append(dot(diagonal, states))
    for load in loads[7:9]:
        load.wait()

    position0 = iota((rows, rows), 0)
    position1 = iota((rows, rows), 1)
    row_of0 = natural_row(position0, grid)
    row_of1 = natural_row(position1, grid)
    to_held = (position0 == row_of1).astype(F32)
    not_after = (row_of0 <= row_of1).astype(BF16)
    expert = iota((8, rows), 0) * (nz // 2) + z // 2
    hit = jnp.zeros((8, rows), jnp.bool_)
    weight = jnp.zeros((8, rows), F32)
    for t in range(routes_ref.shape[0]):
        route = jnp.broadcast_to(routes_ref[t : t + 1, :].astype(F32), (8, rows))
        route = dot(route.astype(BF16), to_held.astype(BF16))
        gate_value = jnp.broadcast_to(weight_ref[t : t + 1, :], (8, rows))
        gate_value = dot(gate_value, to_held, precision=lax.Precision.HIGHEST)
        same = route == expert.astype(F32)
        hit = jnp.logical_or(hit, same)
        weight = weight + jnp.where(same, gate_value, 0.0)
    rank = dot(hit.astype(F32).astype(BF16), not_after)
    rank = jnp.where(hit, rank, 0.0)
    place = (iota((CAPACITY, rows), 0) + 1).astype(F32)
    picks, slot_weights = [], []
    for yy in range(ny):
        chosen = rank[yy : yy + 1, :] == place
        picks.append(chosen.astype(F32))
        slot_weights.append(
            jnp.sum(jnp.where(chosen, weight[yy : yy + 1, :], 0.0), axis=1, keepdims=True)
        )
    pick = jnp.concatenate(picks, axis=0).astype(BF16)
    mine0 = iota((rows // CORES, rows), 0)
    mine0 = (mine0 // half) * (CORES * half) + c * half + mine0 % half
    mine0 = natural_row(mine0, grid)
    from_held = (iota((rows // CORES, rows), 1) == mine0).astype(BF16)

    every1.wait_recv()
    arrived = rcv1[...].astype(F32).reshape(wide, hd).astype(BF16)
    base = jnp.concatenate(base_old, axis=0) + dot(new_q, arrived)
    raw = jnp.exp(-decay_ref[...]) * base + jnp.sum(q * kk, axis=1, keepdims=True) * vv
    power = jnp.mean(raw * raw, axis=1, keepdims=True)
    heads_buf[c, x] = (raw * lax.rsqrt(power + EPSILON)).astype(BF16)

    copies2 = []
    for i, (xx, cc) in enumerate(in_row):
        copy = remote(
            heads_buf.at[c, x], heads_buf.at[c, x], s2.at[i], r2.at[i], at(xx, y, z, cc)
        )
        copy.start()
        copies2.append(copy)
    for load in loads[9:12]:
        load.wait()
    copy_wo.wait_recv()
    for copy in copies2:
        copy.wait_recv()

    heads = jnp.concatenate(
        [dot(from_held, heads_buf[cc].reshape(rows, hd)).astype(BF16) for cc in range(CORES)],
        axis=1,
    )
    row_in_half = iota((half, cols), 0)
    for yy in range(ny):
        columns = slice(yy * cols, (yy + 1) * cols)
        weights = wo_v[:, :, columns].reshape(CORES * hd, cols)
        partial[yy] = dot(heads, weights).reshape(nz, half, cols)
        res = residual_ref[:, columns].astype(F32)
        partial[yy, z] += jnp.where(row_in_half == 2 * y, res[0:1, :], 0.0) + jnp.where(
            row_in_half == 2 * y + 1, res[1:2, :], 0.0
        )
        snd4[yy * nz : (yy + 1) * nz] = partial[yy].astype(BF16)

    for i, (yy, zz) in enumerate(in_plane):
        remote(
            snd4.at[yy * nz + zz], rcv4.at[i], s4.at[0], r4.at[0], at(x, yy, zz, c)
        ).start()
    mine = partial[y, z]
    every4 = all_of(snd4, rcv4, s4.at[0], r4.at[0])
    every4.wait_recv()
    for i in range(plane - 1):
        mine = mine + rcv4[i].astype(F32)
    mixed = mine.astype(BF16)

    full[z, c] = mixed
    copies6 = []
    for i, (zz, cc) in enumerate(in_column):
        copy = remote(full.at[z, c], full.at[z, c], s6.at[i], r6.at[i], at(x, y, zz, cc))
        copy.start()
        copies6.append(copy)
    for copy in copies6:
        copy.wait_recv()

    every_row = full[...].astype(F32).reshape(rows, cols).astype(BF16)
    picked = dot(pick, every_row).astype(BF16)
    for yy in range(ny):
        snd7[yy] = picked[yy * CAPACITY : (yy + 1) * CAPACITY]
    copies7 = []
    for i, (dx, dy) in enumerate(steps_xy):
        xx, yy = step(x, dx, nx), step(y, dy, ny)
        copy = remote(snd7.at[yy], xin.at[here], s7.at[i], r7.at[i], at(xx, yy, z, c))
        copy.start()
        copies7.append(copy)
    xin[here] = snd7[y]
    for load in loads[12:]:
        load.wait()

    def one_block(block, carry):
        gate_sum, up_sum, squares = carry
        taken_rows = xin[block].astype(F32)
        columns = pl.ds(pl.multiple_of(block * cols, cols), cols)
        squares = squares + jnp.sum(taken_rows * taken_rows, axis=1, keepdims=True)
        scaled = (taken_rows * gain_ref[:, columns]).astype(BF16)
        gate_sum = gate_sum + dot(scaled, gate_v[:, columns], ((1,), (1,)))
        up_sum = up_sum + dot(scaled, up_v[:, columns], ((1,), (1,)))
        return gate_sum, up_sum, squares

    hidden_units = gate_v.shape[0]
    carry = (
        jnp.zeros((CAPACITY, hidden_units), F32),
        jnp.zeros((CAPACITY, hidden_units), F32),
        jnp.zeros((CAPACITY, 1), F32),
    )
    carry = one_block(here, carry)
    for i in reversed(range(nx * ny - 1)):
        dx, dy = steps_xy[i]
        copies7[i].wait_recv()
        carry = one_block(step(x, nx - dx, nx) * ny + step(y, ny - dy, ny), carry)
    gate_sum, up_sum, squares = carry
    scale = lax.rsqrt(squares / (nx * ny * cols) + EPSILON)
    gate_sum = gate_sum * scale
    up_sum = up_sum * scale
    hidden = (gate_sum / (1.0 + jnp.exp(-gate_sum)) * up_sum).astype(BF16)

    def down_block(block):
        columns = pl.ds(pl.multiple_of(block * cols, cols), cols)
        return dot(hidden, down_v[:, columns]).astype(BF16)

    copies8 = []
    for i, (dx, dy) in enumerate(steps_xy):
        xx, yy = step(x, dx, nx), step(y, dy, ny)
        snd8[i] = down_block(xx * ny + yy)
        copy = remote(snd8.at[i], rcv8.at[here], s8.at[i], r8.at[i], at(xx, yy, z, c))
        copy.start()
        copies8.append(copy)
    rcv8[here] = down_block(here)
    for copy in copies8:
        copy.wait_recv()

    summed = []
    for yy in range(ny):
        term = rcv8[yy].astype(F32)
        for xx in range(1, nx):
            term = term + rcv8[xx * ny + yy].astype(F32)
        summed.append(term * slot_weights[yy])
    summed = jnp.concatenate(summed, axis=0).astype(BF16)
    routed = dot(pick, summed, ((0,), (0,)))
    own9[...] = routed.reshape(nz, CORES, half, cols)

    snd9[...] = own9[:, 1 - c].astype(BF16)
    copy9 = remote(snd9, rcv9, s9.at[0], r9.at[0], other)
    copy9.start()
    own9[z, c] += mixed.astype(F32)
    copy9.wait_recv()
    for zz in range(nz):
        block = own9[zz, c] + rcv9[zz].astype(F32)
        for yy in range(ny):
            snd10[yy * nz + zz] = block[2 * yy : 2 * yy + 2, :]
    for yy, zz in in_plane:
        remote(
            snd10.at[yy * nz + zz],
            rcv10.at[place_yz],
            s10.at[0],
            r10.at[0],
            at(x, yy, zz, c),
        ).start()
    rcv10[place_yz] = snd10[place_yz]
    every10 = all_of(snd10, rcv10, s10.at[0], r10.at[0])
    every10.wait_recv()
    for yy in range(ny):
        total = rcv10[yy * nz]
        for zz in range(1, nz):
            total = total + rcv10[yy * nz + zz]
        out_ref[:, yy * cols : (yy + 1) * cols] = total.astype(BF16)

    for copy in [copy_wo, every1, every4, copy9, every10]:
        copy.wait_send()
    for copy in copies2 + copies6 + copies7 + copies8:
        copy.wait_send()


def body(
    grid,
    residual_in,
    queries,
    keys_new,
    values_new,
    cached_state,
    incoming_state,
    admit_slot,
    occupancy,
    decay_rate,
    out_proj,
    norm_gain,
    routes,
    route_weight,
    gate_proj,
    up_proj,
    down_proj,
):
    nx, ny, nz = grid
    slots, hd = queries.shape
    rows = nx * slots
    half = 2 * ny
    plane = ny * nz
    cols = residual_in.shape[1] // ny
    blocks = nx * ny
    units = gate_proj.shape[2]
    width = gate_proj.shape[1]
    admitted, parts, kb, _ = incoming_state.shape

    vmem = pl.BlockSpec(memory_space=pltpu.VMEM)
    anywhere = pl.BlockSpec(memory_space=pl.ANY)
    dma = lambda n: pltpu.SemaphoreType.DMA((n,))
    scratch = [
        pltpu.VMEM((parts, admitted * kb, hd), F32),
        pltpu.SMEM(admit_slot.shape, jnp.int32),
        pltpu.VMEM((1, slots), jnp.int32),
        pltpu.VMEM((slots, hd), BF16),
        pltpu.VMEM((slots, hd), BF16),
        pltpu.VMEM((slots, hd), BF16),
        pltpu.VMEM((1, 1), F32),
        pltpu.VMEM((routes.shape[1], rows), jnp.int32),
        pltpu.VMEM((routes.shape[1], rows), F32),
        pltpu.VMEM(residual_in.shape, BF16),
        pltpu.VMEM((1, width), F32),
        pltpu.VMEM((slots * hd, hd), F32),
        pltpu.VMEM((CORES,) + out_proj.shape, BF16),
        pltpu.VMEM((units, width), BF16),
        pltpu.VMEM((units, width), BF16),
        pltpu.VMEM((units, width), BF16),
        pltpu.VMEM((parts, admitted * kb, hd), BF16),
        pltpu.VMEM((parts, admitted * kb, hd), BF16),
        pltpu.VMEM((CORES, nx, slots, hd), BF16),
        pltpu.VMEM((ny, nz, half, cols), F32),
        pltpu.VMEM((plane, half, cols), BF16),
        pltpu.VMEM((plane, half, cols), BF16),
        pltpu.VMEM((nz, CORES, half, cols), BF16),
        pltpu.VMEM((ny, CAPACITY, cols), BF16),
        pltpu.VMEM((blocks, CAPACITY, cols), BF16),
        pltpu.VMEM((blocks, CAPACITY, cols), BF16),
        pltpu.VMEM((blocks, CAPACITY, cols), BF16),
        pltpu.VMEM((nz, CORES, half, cols), F32),
        pltpu.VMEM((nz, half, cols), BF16),
        pltpu.VMEM((nz, half, cols), BF16),
        pltpu.VMEM((plane, 2, cols), F32),
        pltpu.VMEM((plane, 2, cols), F32),
        dma(admitted + 15),
    ]
    for n in (1, nx * CORES - 1, 1, 1, nz * CORES - 1, blocks - 1, blocks - 1, 1, 1):
        scratch += [dma(n), dma(n)]

    def kernel(*refs):
        layer_kernel(grid, refs[:16], *refs[16:])

    return pl.pallas_call(
        kernel,
        out_shape=pltpu.VMEM(residual_in.shape, BF16),
        in_specs=[anywhere] * 16,
        out_specs=vmem,
        scratch_shapes=scratch,
        compiler_params=pltpu.CompilerParams(
            collective_id=0, has_side_effects=True, vmem_limit_bytes=VMEM_BYTES
        ),
    )(
        incoming_state,
        admit_slot,
        occupancy.reshape(1, slots),
        queries,
        keys_new,
        values_new,
        decay_rate.reshape(1, 1),
        cached_state.reshape(slots * hd, hd),
        routes.T,
        route_weight.T,
        residual_in,
        out_proj,
        norm_gain.reshape(1, width),
        gate_proj[0].T,
        up_proj[0].T,
        down_proj[0],
    )


def solution(mesh):
    in_specs = (
        P("ep", "sec"),
        P("sec", "ep"),
        P("sec", "ep"),
        P("sec", "ep"),
        P("sec", "ep", None, None),
        P("sec", None, "ep", None),
        P("sec"),
        P("sec"),
        P("ep"),
        P("ep", "sec"),
        P(),
        P(),
        P(),
        P("ep", None, "sec"),
        P("ep", None, "sec"),
        P("ep", "sec", None),
    )
    return jax.shard_map(
        functools.partial(body, GRID),
        mesh=mesh,
        in_specs=in_specs,
        out_specs=P("ep", "sec"),
        check_vma=False,
    )
```

```python
import functools

import jax
import jax.numpy as jnp
from jax import lax
from jax.experimental import pallas as pl
from jax.experimental.pallas import tpu as pltpu
from jax.sharding import PartitionSpec as P

EPSILON = 1e-06
CORES = 2
CAPACITY = 32
VMEM_BYTES = 62 * 2**20
MESH = pl.DeviceIdType.MESH
F32 = jnp.float32
BF16 = jnp.bfloat16
GRID = (4, 4, 8)


def iota(shape, dim):
    return lax.broadcasted_iota(jnp.int32, shape, dim)


def natural_row(position, grid):
    _, ny, nz = grid
    half = 2 * ny
    zi = position // (CORES * half)
    ci = (position // half) % CORES
    yi = (position % half) // 2
    return (yi * nz + zi) * (2 * CORES) + ci * 2 + position % 2


def far_first(*sizes):
    steps = [()]
    for size in sizes:
        steps = [step + (i,) for step in steps for i in range(size)]

    def distance(step):
        return sum(min(i, size - i) for i, size in zip(step, sizes))

    return sorted(steps, key=lambda step: -distance(step))[:-1]


def dot(a, b, dims=((1,), (0,)), precision=None):
    return lax.dot_general(a, b, (dims, ((), ())), preferred_element_type=F32, precision=precision)


def layer_kernel(
    grid,
    operands,
    out_ref,
    incoming_v,
    admit_ref,
    occupancy_ref,
    q_ref,
    k_ref,
    v_ref,
    decay_ref,
    routes_ref,
    weight_ref,
    residual_ref,
    gain_ref,
    state_v,
    wo_v,
    gate_v,
    up_v,
    down_v,
    gate_t,
    up_t,
    snd1,
    rcv1,
    heads_buf,
    partial,
    snd4,
    rcv4,
    full,
    pick_buf,
    snd7,
    xin,
    snd8,
    rcv8,
    own9,
    snd9,
    rcv9,
    snd10,
    rcv10,
    local_sem,
    s1,
    r1,
    s2,
    r2,
    s3,
    r3,
    s4,
    r4,
    s6,
    r6,
    s7,
    r7,
    s8,
    r8,
    s9,
    r9,
    s10,
    r10,
):
    nx, ny, nz = grid
    slots, hd = q_ref.shape
    parts = ny * nz * CORES
    kb = hd // parts
    rows = nx * slots
    half = 2 * ny
    plane = ny * nz
    cols = xin.shape[2]
    admitted = admit_ref.shape[0]
    wide = parts * admitted * kb

    x = lax.axis_index("sec")
    ep = lax.axis_index("ep")
    c = lax.rem(ep, CORES)
    z = lax.rem(ep // CORES, nz)
    y = ep // (CORES * nz)

    here = x * ny + y
    place_yz = y * nz + z

    def at(xx, yy, zz, cc):
        return (xx, (yy * nz + zz) * CORES + cc)

    def remote(src, dst, send_sem, recv_sem, device):
        return pltpu.make_async_remote_copy(
            src, dst, send_sem, recv_sem, device_id=device, device_id_type=MESH
        )

    def step(start, by, size):
        return lax.rem(start + by, size)

    other = at(x, y, z, 1 - c)
    in_ep = [
        (step(y, dy, ny), step(z, dz, nz), step(c, dc, CORES))
        for dy, dz, dc in far_first(ny, nz, CORES)
    ]
    in_plane = [(step(y, dy, ny), step(z, dz, nz)) for dy, dz in far_first(ny, nz)]
    in_column = [(step(z, dz, nz), step(c, dc, CORES)) for dz, dc in far_first(nz, CORES)]
    in_row = [(step(x, dx, nx), step(c, dc, CORES)) for dx, dc in far_first(nx, CORES)]
    steps_xy = far_first(nx, ny)

    def all_of(src, dst, send_sem, recv_sem):
        count = plane - 1
        return remote(
            src.at[pl.ds(0, count)], dst.at[pl.ds(0, count)], send_sem, recv_sem, other
        )

    incoming_hbm, *others = operands
    held = (
        admit_ref,
        occupancy_ref,
        q_ref,
        k_ref,
        v_ref,
        decay_ref,
        state_v,
        routes_ref,
        weight_ref,
        residual_ref,
        wo_v.at[c],
        gain_ref,
        gate_v,
        up_v,
        down_v,
    )
    incoming_loads = [
        pltpu.make_async_copy(
            incoming_hbm.at[a], incoming_v.at[:, kb * a : kb * (a + 1), :], local_sem.at[a]
        )
        for a in range(admitted)
    ]
    loads = [
        pltpu.make_async_copy(src, dst, local_sem.at[admitted + i])
        for i, (src, dst) in enumerate(zip(others, held))
    ]
    for load in incoming_loads + loads:
        load.start()

    barrier = pltpu.get_barrier_semaphore()
    partners = [at(x, yy, zz, cc) for yy, zz, cc in in_ep]
    partners += [
        at(step(x, dx, nx), step(y, dy, ny), z, c) for dx, dy in far_first(nx, ny) if dx
    ]
    partners += [at(xx, y, z, 1 - c) for xx in [step(x, dx, nx) for dx in range(1, nx)]]
    for partner in partners:
        pl.semaphore_signal(barrier, inc=1, device_id=partner, device_id_type=MESH)

    for load in incoming_loads:
        load.wait()
    snd1[...] = incoming_v[...].astype(BF16)
    pl.semaphore_wait(barrier, len(partners))
    wo_hbm = others[10]
    copy_wo = remote(wo_hbm, wo_v.at[c], s3.at[0], r3.at[0], other)
    for yy, zz, cc in in_ep:
        remote(
            snd1.at[(yy * nz + zz) * CORES + cc],
            rcv1.at[ep],
            s1.at[0],
            r1.at[0],
            at(x, yy, zz, cc),
        ).start()
    rcv1[ep] = snd1[ep]
    copy_wo.start()
    every1 = remote(
        snd1.at[pl.ds(0, parts - 1)],
        rcv1.at[pl.ds(0, parts - 1)],
        s1.at[0],
        r1.at[0],
        other,
    )

    for load in loads[:7]:
        load.wait()

    q = q_ref[...].astype(F32)
    kk = k_ref[...].astype(F32)
    vv = v_ref[...].astype(F32)
    occupancy = occupancy_ref[...].astype(F32)
    eye = iota((slots, slots), 0) == iota((slots, slots), 1)
    kept = jnp.sum(jnp.where(eye, occupancy, 0.0), axis=1, keepdims=True)
    slot_row = iota((slots, 1), 0)
    taken = jnp.zeros((slots, 1), jnp.bool_)
    lane = iota((1, wide), 1)
    lane_request = (lane // kb) % admitted
    lane_slot = jnp.zeros((1, wide), jnp.int32)
    for a in range(admitted):
        slot = admit_ref[a] - x * slots
        taken = jnp.logical_or(taken, slot_row == slot)
        lane_slot = jnp.where(lane_request == a, slot, lane_slot)
    old_q = jnp.where(taken, 0.0, q * kept)
    lane2 = iota((hd, wide), 1)
    spread_key = (lane2 // (admitted * kb)) * kb + lane2 % kb
    repeat = (iota((hd, wide), 0) == spread_key).astype(BF16)
    new_q = dot(q.astype(BF16), repeat)
    new_q = jnp.where(slot_row == lane_slot, new_q, 0.0).astype(BF16)
    base_old = []
    row8 = iota((8, hd), 0)
    for chunk in range(slots // 8):
        part = old_q[chunk * 8 : chunk * 8 + 8]
        diagonal = jnp.concatenate(
            [jnp.where(row8 == s, part, 0.0) for s in range(8)], axis=1
        ).astype(BF16)
        states = state_v[chunk * 8 * hd : (chunk + 1) * 8 * hd, :].astype(BF16)
        base_old.append(dot(diagonal, states))
    for load in loads[7:9]:
        load.wait()

    position0 = iota((rows, rows), 0)
    position1 = iota((rows, rows), 1)
    row_of0 = natural_row(position0, grid)
    row_of1 = natural_row(position1, grid)
    to_held = (position0 == row_of1).astype(F32)
    not_after = (row_of0 <= row_of1).astype(BF16)
    expert = iota((8, rows), 0) * (nz // 2) + z // 2
    hit = jnp.zeros((8, rows), jnp.bool_)
    weight = jnp.zeros((8, rows), F32)
    for t in range(routes_ref.shape[0]):
        route = jnp.broadcast_to(routes_ref[t : t + 1, :].astype(F32), (8, rows))
        route = dot(route.astype(BF16), to_held.astype(BF16))
        gate_value = jnp.broadcast_to(weight_ref[t : t + 1, :], (8, rows))
        gate_value = dot(gate_value, to_held, precision=lax.Precision.HIGHEST)
        same = route == expert.astype(F32)
        hit = jnp.logical_or(hit, same)
        weight = weight + jnp.where(same, gate_value, 0.0)
    rank = dot(hit.astype(F32).astype(BF16), not_after)
    rank = jnp.where(hit, rank, 0.0)
    place = (iota((CAPACITY, rows), 0) + 1).astype(F32)
    picks, slot_weights = [], []
    for yy in range(ny):
        chosen = rank[yy : yy + 1, :] == place
        picks.append(chosen.astype(F32))
        slot_weights.append(
            jnp.sum(jnp.where(chosen, weight[yy : yy + 1, :], 0.0), axis=1, keepdims=True)
        )
    pick = jnp.concatenate(picks, axis=0).astype(BF16)
    for yy in range(ny):
        pick_buf[yy] = picks[yy].astype(BF16)
    mine0 = iota((rows // CORES, rows), 0)
    mine0 = (mine0 // half) * (CORES * half) + c * half + mine0 % half
    mine0 = natural_row(mine0, grid)
    from_held = (iota((rows // CORES, rows), 1) == mine0).astype(BF16)

    every1.wait_recv()
    arrived = rcv1[...].astype(F32).reshape(wide, hd).astype(BF16)
    base = jnp.concatenate(base_old, axis=0) + dot(new_q, arrived)
    raw = jnp.exp(-decay_ref[...]) * base + jnp.sum(q * kk, axis=1, keepdims=True) * vv
    power = jnp.mean(raw * raw, axis=1, keepdims=True)
    heads_buf[c, x] = (raw * lax.rsqrt(power + EPSILON)).astype(BF16)

    copies2 = []
    for i, (xx, cc) in enumerate(in_row):
        copy = remote(
            heads_buf.at[c, x], heads_buf.at[c, x], s2.at[i], r2.at[i], at(xx, y, z, cc)
        )
        copy.start()
        copies2.append(copy)
    for load in loads[9:12]:
        load.wait()
    copy_wo.wait_recv()
    for copy in copies2:
        copy.wait_recv()

    heads = jnp.concatenate(
        [dot(from_held, heads_buf[cc].reshape(rows, hd)).astype(BF16) for cc in range(CORES)],
        axis=1,
    )
    row_in_half = iota((half, cols), 0)
    for yy in range(ny):
        columns = slice(yy * cols, (yy + 1) * cols)
        weights = wo_v[:, :, columns].reshape(CORES * hd, cols)
        partial[yy] = dot(heads, weights).reshape(nz, half, cols)
        res = residual_ref[:, columns].astype(F32)
        partial[yy, z] += jnp.where(row_in_half == 2 * y, res[0:1, :], 0.0) + jnp.where(
            row_in_half == 2 * y + 1, res[1:2, :], 0.0
        )
        snd4[yy * nz : (yy + 1) * nz] = partial[yy].astype(BF16)

    for i, (yy, zz) in enumerate(in_plane):
        remote(
            snd4.at[yy * nz + zz], rcv4.at[i], s4.at[0], r4.at[0], at(x, yy, zz, c)
        ).start()
    mine = partial[y, z]
    every4 = all_of(snd4, rcv4, s4.at[0], r4.at[0])
    for load in loads[12:14]:
        load.wait()
    for block in range(nx * ny):
        columns = slice(block * cols, (block + 1) * cols)
        gate_t[columns, :] = gate_v[:, columns].T
        up_t[columns, :] = up_v[:, columns].T
    every4.wait_recv()
    for i in range(plane - 1):
        mine = mine + rcv4[i].astype(F32)
    mixed = mine.astype(BF16)

    full[z, c] = mixed
    copies6 = []
    for i, (zz, cc) in enumerate(in_column):
        copy = remote(full.at[z, c], full.at[z, c], s6.at[i], r6.at[i], at(x, y, zz, cc))
        copy.start()
        copies6.append(copy)
    for copy in copies6:
        copy.wait_recv()

    every_row = full[...].astype(F32).reshape(rows, cols).astype(BF16)
    for dy in [dy for (dy,) in far_first(ny)] + [0]:
        yy = step(y, dy, ny)
        snd7[yy] = dot(pick_buf[yy], every_row).astype(BF16)
        for i, (dx, dyy) in enumerate(steps_xy):
            if dyy == dy:
                remote(
                    snd7.at[yy],
                    xin.at[here],
                    s7.at[i],
                    r7.at[i],
                    at(step(x, dx, nx), yy, z, c),
                ).start()
    copies7 = []
    for i, (dx, dy) in enumerate(steps_xy):
        xx, yy = step(x, dx, nx), step(y, dy, ny)
        copy = remote(snd7.at[yy], xin.at[here], s7.at[i], r7.at[i], at(xx, yy, z, c))
        copies7.append(copy)
    xin[here] = snd7[y]
    loads[14].wait()

    def one_block(block, carry):
        gate_sum, up_sum, squares = carry
        taken_rows = xin[block].astype(F32)
        columns = pl.ds(pl.multiple_of(block * cols, cols), cols)
        squares = squares + jnp.sum(taken_rows * taken_rows, axis=1, keepdims=True)
        scaled = (taken_rows * gain_ref[:, columns]).astype(BF16)
        gate_sum = gate_sum + dot(scaled, gate_t[columns, :])
        up_sum = up_sum + dot(scaled, up_t[columns, :])
        return gate_sum, up_sum, squares

    hidden_units = gate_v.shape[0]
    carry = (
        jnp.zeros((CAPACITY, hidden_units), F32),
        jnp.zeros((CAPACITY, hidden_units), F32),
        jnp.zeros((CAPACITY, 1), F32),
    )
    carry = one_block(here, carry)
    for i in range(nx * ny - 1):
        dx, dy = steps_xy[i]
        copies7[i].wait_recv()
        carry = one_block(step(x, nx - dx, nx) * ny + step(y, ny - dy, ny), carry)
    gate_sum, up_sum, squares = carry
    scale = lax.rsqrt(squares / (nx * ny * cols) + EPSILON)
    gate_sum = gate_sum * scale
    up_sum = up_sum * scale
    hidden = (gate_sum / (1.0 + jnp.exp(-gate_sum)) * up_sum).astype(BF16)

    def down_block(block):
        columns = pl.ds(pl.multiple_of(block * cols, cols), cols)
        return dot(hidden, down_v[:, columns]).astype(BF16)

    copies8 = []
    for i, (dx, dy) in enumerate(steps_xy):
        xx, yy = step(x, dx, nx), step(y, dy, ny)
        snd8[i] = down_block(xx * ny + yy)
        copy = remote(snd8.at[i], rcv8.at[here], s8.at[i], r8.at[i], at(xx, yy, z, c))
        copy.start()
        copies8.append(copy)
    rcv8[here] = down_block(here)
    for copy in copies8:
        copy.wait_recv()

    summed = []
    for yy in range(ny):
        term = rcv8[yy].astype(F32)
        for xx in range(1, nx):
            term = term + rcv8[xx * ny + yy].astype(F32)
        summed.append(term * slot_weights[yy])
    summed = jnp.concatenate(summed, axis=0).astype(BF16)
    routed = dot(pick, summed, ((0,), (0,)))
    own9[...] = routed.reshape(nz, CORES, half, cols)

    snd9[...] = own9[:, 1 - c].astype(BF16)
    copy9 = remote(snd9, rcv9, s9.at[0], r9.at[0], other)
    copy9.start()
    own9[z, c] += mixed.astype(F32)
    copy9.wait_recv()
    for zz in range(nz):
        block = own9[zz, c] + rcv9[zz].astype(F32)
        for yy in range(ny):
            snd10[yy * nz + zz] = block[2 * yy : 2 * yy + 2, :]
    for yy, zz in in_plane:
        remote(
            snd10.at[yy * nz + zz],
            rcv10.at[place_yz],
            s10.at[0],
            r10.at[0],
            at(x, yy, zz, c),
        ).start()
    rcv10[place_yz] = snd10[place_yz]
    every10 = all_of(snd10, rcv10, s10.at[0], r10.at[0])
    every10.wait_recv()
    for yy in range(ny):
        total = rcv10[yy * nz]
        for zz in range(1, nz):
            total = total + rcv10[yy * nz + zz]
        out_ref[:, yy * cols : (yy + 1) * cols] = total.astype(BF16)

    for copy in [copy_wo, every1, every4, copy9, every10]:
        copy.wait_send()
    for copy in copies2 + copies6 + copies7 + copies8:
        copy.wait_send()


def body(
    grid,
    residual_in,
    queries,
    keys_new,
    values_new,
    cached_state,
    incoming_state,
    admit_slot,
    occupancy,
    decay_rate,
    out_proj,
    norm_gain,
    routes,
    route_weight,
    gate_proj,
    up_proj,
    down_proj,
):
    nx, ny, nz = grid
    slots, hd = queries.shape
    rows = nx * slots
    half = 2 * ny
    plane = ny * nz
    cols = residual_in.shape[1] // ny
    blocks = nx * ny
    units = gate_proj.shape[2]
    width = gate_proj.shape[1]
    admitted, parts, kb, _ = incoming_state.shape

    vmem = pl.BlockSpec(memory_space=pltpu.VMEM)
    anywhere = pl.BlockSpec(memory_space=pl.ANY)
    dma = lambda n: pltpu.SemaphoreType.DMA((n,))
    scratch = [
        pltpu.VMEM((parts, admitted * kb, hd), F32),
        pltpu.SMEM(admit_slot.shape, jnp.int32),
        pltpu.VMEM((1, slots), jnp.int32),
        pltpu.VMEM((slots, hd), BF16),
        pltpu.VMEM((slots, hd), BF16),
        pltpu.VMEM((slots, hd), BF16),
        pltpu.VMEM((1, 1), F32),
        pltpu.VMEM((routes.shape[1], rows), jnp.int32),
        pltpu.VMEM((routes.shape[1], rows), F32),
        pltpu.VMEM(residual_in.shape, BF16),
        pltpu.VMEM((1, width), F32),
        pltpu.VMEM((slots * hd, hd), F32),
        pltpu.VMEM((CORES,) + out_proj.shape, BF16),
        pltpu.VMEM((units, width), BF16),
        pltpu.VMEM((units, width), BF16),
        pltpu.VMEM((units, width), BF16),
        pltpu.VMEM((width, units), BF16),
        pltpu.VMEM((width, units), BF16),
        pltpu.VMEM((parts, admitted * kb, hd), BF16),
        pltpu.VMEM((parts, admitted * kb, hd), BF16),
        pltpu.VMEM((CORES, nx, slots, hd), BF16),
        pltpu.VMEM((ny, nz, half, cols), F32),
        pltpu.VMEM((plane, half, cols), BF16),
        pltpu.VMEM((plane, half, cols), BF16),
        pltpu.VMEM((nz, CORES, half, cols), BF16),
        pltpu.VMEM((ny, CAPACITY, rows), BF16),
        pltpu.VMEM((ny, CAPACITY, cols), BF16),
        pltpu.VMEM((blocks, CAPACITY, cols), BF16),
        pltpu.VMEM((blocks, CAPACITY, cols), BF16),
        pltpu.VMEM((blocks, CAPACITY, cols), BF16),
        pltpu.VMEM((nz, CORES, half, cols), F32),
        pltpu.VMEM((nz, half, cols), BF16),
        pltpu.VMEM((nz, half, cols), BF16),
        pltpu.VMEM((plane, 2, cols), F32),
        pltpu.VMEM((plane, 2, cols), F32),
        dma(admitted + 15),
    ]
    for n in (1, nx * CORES - 1, 1, 1, nz * CORES - 1, blocks - 1, blocks - 1, 1, 1):
        scratch += [dma(n), dma(n)]

    def kernel(*refs):
        layer_kernel(grid, refs[:16], *refs[16:])

    return pl.pallas_call(
        kernel,
        out_shape=pltpu.VMEM(residual_in.shape, BF16),
        in_specs=[anywhere] * 16,
        out_specs=vmem,
        scratch_shapes=scratch,
        compiler_params=pltpu.CompilerParams(
            collective_id=0, has_side_effects=True, vmem_limit_bytes=VMEM_BYTES
        ),
    )(
        incoming_state,
        admit_slot,
        occupancy.reshape(1, slots),
        queries,
        keys_new,
        values_new,
        decay_rate.reshape(1, 1),
        cached_state.reshape(slots * hd, hd),
        routes.T,
        route_weight.T,
        residual_in,
        out_proj,
        norm_gain.reshape(1, width),
        gate_proj[0].T,
        up_proj[0].T,
        down_proj[0],
    )


def solution(mesh):
    in_specs = (
        P("ep", "sec"),
        P("sec", "ep"),
        P("sec", "ep"),
        P("sec", "ep"),
        P("sec", "ep", None, None),
        P("sec", None, "ep", None),
        P("sec"),
        P("sec"),
        P("ep"),
        P("ep", "sec"),
        P(),
        P(),
        P(),
        P("ep", None, "sec"),
        P("ep", None, "sec"),
        P("ep", "sec", None),
    )
    return jax.shard_map(
        functools.partial(body, GRID),
        mesh=mesh,
        in_specs=in_specs,
        out_specs=P("ep", "sec"),
        check_vma=False,
    )
```

```python
import functools

import jax
import jax.numpy as jnp
from jax import lax
from jax.experimental import pallas as pl
from jax.experimental.pallas import tpu as pltpu
from jax.sharding import PartitionSpec as P

EPSILON = 1e-06
CORES = 2
CAPACITY = 32
VMEM_BYTES = 62 * 2**20
MESH = pl.DeviceIdType.MESH
F32 = jnp.float32
BF16 = jnp.bfloat16
GRID = (4, 4, 8)


def iota(shape, dim):
    return lax.broadcasted_iota(jnp.int32, shape, dim)


def natural_row(position, grid):
    _, ny, nz = grid
    half = 2 * ny
    zi = position // (CORES * half)
    ci = (position // half) % CORES
    yi = (position % half) // 2
    return (yi * nz + zi) * (2 * CORES) + ci * 2 + position % 2


def far_first(*sizes):
    steps = [()]
    for size in sizes:
        steps = [step + (i,) for step in steps for i in range(size)]

    def distance(step):
        return sum(min(i, size - i) for i, size in zip(step, sizes))

    return sorted(steps, key=lambda step: -distance(step))[:-1]


def dot(a, b, dims=((1,), (0,)), precision=None):
    return lax.dot_general(a, b, (dims, ((), ())), preferred_element_type=F32, precision=precision)


def layer_kernel(
    grid,
    operands,
    out_ref,
    incoming_v,
    admit_ref,
    occupancy_ref,
    q_ref,
    k_ref,
    v_ref,
    decay_ref,
    routes_ref,
    weight_ref,
    residual_ref,
    gain_ref,
    state_v,
    wo_v,
    gate_v,
    up_v,
    down_v,
    gate_t,
    up_t,
    snd1,
    rcv1,
    heads_buf,
    partial,
    snd4,
    rcv4,
    full,
    pick_buf,
    snd7,
    xin,
    snd8,
    rcv8,
    own9,
    snd9,
    rcv9,
    snd10,
    rcv10,
    local_sem,
    s1,
    r1,
    s2,
    r2,
    s3,
    r3,
    s4,
    r4,
    s6,
    r6,
    s7,
    r7,
    s8,
    r8,
    s9,
    r9,
    s10,
    r10,
):
    nx, ny, nz = grid
    slots, hd = q_ref.shape
    parts = ny * nz * CORES
    kb = hd // parts
    rows = nx * slots
    half = 2 * ny
    plane = ny * nz
    cols = xin.shape[2]
    admitted = admit_ref.shape[0]
    wide = parts * admitted * kb

    x = lax.axis_index("sec")
    ep = lax.axis_index("ep")
    c = lax.rem(ep, CORES)
    z = lax.rem(ep // CORES, nz)
    y = ep // (CORES * nz)

    here = x * ny + y
    place_yz = y * nz + z

    def at(xx, yy, zz, cc):
        return (xx, (yy * nz + zz) * CORES + cc)

    def remote(src, dst, send_sem, recv_sem, device):
        return pltpu.make_async_remote_copy(
            src, dst, send_sem, recv_sem, device_id=device, device_id_type=MESH
        )

    def step(start, by, size):
        return lax.rem(start + by, size)

    other = at(x, y, z, 1 - c)
    in_ep = [
        (step(y, dy, ny), step(z, dz, nz), step(c, dc, CORES))
        for dy, dz, dc in far_first(ny, nz, CORES)
    ]
    in_plane = [(step(y, dy, ny), step(z, dz, nz)) for dy, dz in far_first(ny, nz)]
    in_column = [(step(z, dz, nz), step(c, dc, CORES)) for dz, dc in far_first(nz, CORES)]
    in_row = [(step(x, dx, nx), step(c, dc, CORES)) for dx, dc in far_first(nx, CORES)]
    steps_xy = sorted(far_first(nx, ny), key=lambda d: -(min(d[0], nx - d[0]) + 2 * min(d[1], ny - d[1])))

    def all_of(src, dst, send_sem, recv_sem):
        count = plane - 1
        return remote(
            src.at[pl.ds(0, count)], dst.at[pl.ds(0, count)], send_sem, recv_sem, other
        )

    incoming_hbm, *others = operands
    held = (
        admit_ref,
        occupancy_ref,
        q_ref,
        k_ref,
        v_ref,
        decay_ref,
        state_v,
        routes_ref,
        weight_ref,
        residual_ref,
        wo_v.at[c],
        gain_ref,
        gate_v,
        up_v,
        down_v,
    )
    incoming_loads = [
        pltpu.make_async_copy(
            incoming_hbm.at[a], incoming_v.at[:, kb * a : kb * (a + 1), :], local_sem.at[a]
        )
        for a in range(admitted)
    ]
    loads = [
        pltpu.make_async_copy(src, dst, local_sem.at[admitted + i])
        for i, (src, dst) in enumerate(zip(others, held))
    ]
    for load in incoming_loads + loads:
        load.start()

    barrier = pltpu.get_barrier_semaphore()
    partners = [at(x, yy, zz, cc) for yy, zz, cc in in_ep]
    partners += [
        at(step(x, dx, nx), step(y, dy, ny), z, c) for dx, dy in far_first(nx, ny) if dx
    ]
    partners += [at(xx, y, z, 1 - c) for xx in [step(x, dx, nx) for dx in range(1, nx)]]
    for partner in partners:
        pl.semaphore_signal(barrier, inc=1, device_id=partner, device_id_type=MESH)

    for load in incoming_loads:
        load.wait()
    snd1[...] = incoming_v[...].astype(BF16)
    pl.semaphore_wait(barrier, len(partners))
    wo_hbm = others[10]
    copy_wo = remote(wo_hbm, wo_v.at[c], s3.at[0], r3.at[0], other)
    for yy, zz, cc in in_ep:
        remote(
            snd1.at[(yy * nz + zz) * CORES + cc],
            rcv1.at[ep],
            s1.at[0],
            r1.at[0],
            at(x, yy, zz, cc),
        ).start()
    rcv1[ep] = snd1[ep]
    copy_wo.start()
    every1 = remote(
        snd1.at[pl.ds(0, parts - 1)],
        rcv1.at[pl.ds(0, parts - 1)],
        s1.at[0],
        r1.at[0],
        other,
    )

    for load in loads[:7]:
        load.wait()

    q = q_ref[...].astype(F32)
    kk = k_ref[...].astype(F32)
    vv = v_ref[...].astype(F32)
    occupancy = occupancy_ref[...].astype(F32)
    eye = iota((slots, slots), 0) == iota((slots, slots), 1)
    kept = jnp.sum(jnp.where(eye, occupancy, 0.0), axis=1, keepdims=True)
    slot_row = iota((slots, 1), 0)
    taken = jnp.zeros((slots, 1), jnp.bool_)
    lane = iota((1, wide), 1)
    lane_request = (lane // kb) % admitted
    lane_slot = jnp.zeros((1, wide), jnp.int32)
    for a in range(admitted):
        slot = admit_ref[a] - x * slots
        taken = jnp.logical_or(taken, slot_row == slot)
        lane_slot = jnp.where(lane_request == a, slot, lane_slot)
    old_q = jnp.where(taken, 0.0, q * kept)
    lane2 = iota((hd, wide), 1)
    spread_key = (lane2 // (admitted * kb)) * kb + lane2 % kb
    repeat = (iota((hd, wide), 0) == spread_key).astype(BF16)
    new_q = dot(q.astype(BF16), repeat)
    new_q = jnp.where(slot_row == lane_slot, new_q, 0.0).astype(BF16)
    base_old = []
    row8 = iota((8, hd), 0)
    for chunk in range(slots // 8):
        part = old_q[chunk * 8 : chunk * 8 + 8]
        diagonal = jnp.concatenate(
            [jnp.where(row8 == s, part, 0.0) for s in range(8)], axis=1
        ).astype(BF16)
        states = state_v[chunk * 8 * hd : (chunk + 1) * 8 * hd, :].astype(BF16)
        base_old.append(dot(diagonal, states))
    for load in loads[7:9]:
        load.wait()

    position0 = iota((rows, rows), 0)
    position1 = iota((rows, rows), 1)
    row_of0 = natural_row(position0, grid)
    row_of1 = natural_row(position1, grid)
    to_held = (position0 == row_of1).astype(F32)
    not_after = (row_of0 <= row_of1).astype(BF16)
    expert = iota((8, rows), 0) * (nz // 2) + z // 2
    hit = jnp.zeros((8, rows), jnp.bool_)
    weight = jnp.zeros((8, rows), F32)
    for t in range(routes_ref.shape[0]):
        route = jnp.broadcast_to(routes_ref[t : t + 1, :].astype(F32), (8, rows))
        route = dot(route.astype(BF16), to_held.astype(BF16))
        gate_value = jnp.broadcast_to(weight_ref[t : t + 1, :], (8, rows))
        gate_value = dot(gate_value, to_held, precision=lax.Precision.HIGHEST)
        same = route == expert.astype(F32)
        hit = jnp.logical_or(hit, same)
        weight = weight + jnp.where(same, gate_value, 0.0)
    rank = dot(hit.astype(F32).astype(BF16), not_after)
    rank = jnp.where(hit, rank, 0.0)
    place = (iota((CAPACITY, rows), 0) + 1).astype(F32)
    picks, slot_weights = [], []
    for yy in range(ny):
        chosen = rank[yy : yy + 1, :] == place
        picks.append(chosen.astype(F32))
        slot_weights.append(
            jnp.sum(jnp.where(chosen, weight[yy : yy + 1, :], 0.0), axis=1, keepdims=True)
        )
    pick = jnp.concatenate(picks, axis=0).astype(BF16)
    for yy in range(ny):
        pick_buf[yy] = picks[yy].astype(BF16)
    mine0 = iota((rows // CORES, rows), 0)
    mine0 = (mine0 // half) * (CORES * half) + c * half + mine0 % half
    mine0 = natural_row(mine0, grid)
    from_held = (iota((rows // CORES, rows), 1) == mine0).astype(BF16)

    every1.wait_recv()
    arrived = rcv1[...].astype(F32).reshape(wide, hd).astype(BF16)
    base = jnp.concatenate(base_old, axis=0) + dot(new_q, arrived)
    raw = jnp.exp(-decay_ref[...]) * base + jnp.sum(q * kk, axis=1, keepdims=True) * vv
    power = jnp.mean(raw * raw, axis=1, keepdims=True)
    heads_buf[c, x] = (raw * lax.rsqrt(power + EPSILON)).astype(BF16)

    copies2 = []
    for i, (xx, cc) in enumerate(in_row):
        copy = remote(
            heads_buf.at[c, x], heads_buf.at[c, x], s2.at[i], r2.at[i], at(xx, y, z, cc)
        )
        copy.start()
        copies2.append(copy)
    for load in loads[9:12]:
        load.wait()
    copy_wo.wait_recv()
    for copy in copies2:
        copy.wait_recv()

    heads = jnp.concatenate(
        [dot(from_held, heads_buf[cc].reshape(rows, hd)).astype(BF16) for cc in range(CORES)],
        axis=1,
    )
    row_in_half = iota((half, cols), 0)
    for yy in range(ny):
        columns = slice(yy * cols, (yy + 1) * cols)
        weights = wo_v[:, :, columns].reshape(CORES * hd, cols)
        partial[yy] = dot(heads, weights).reshape(nz, half, cols)
        res = residual_ref[:, columns].astype(F32)
        partial[yy, z] += jnp.where(row_in_half == 2 * y, res[0:1, :], 0.0) + jnp.where(
            row_in_half == 2 * y + 1, res[1:2, :], 0.0
        )
        snd4[yy * nz : (yy + 1) * nz] = partial[yy].astype(BF16)

    for i, (yy, zz) in enumerate(in_plane):
        remote(
            snd4.at[yy * nz + zz], rcv4.at[i], s4.at[0], r4.at[0], at(x, yy, zz, c)
        ).start()
    mine = partial[y, z]
    every4 = all_of(snd4, rcv4, s4.at[0], r4.at[0])
    for load in loads[12:14]:
        load.wait()
    for block in range(nx * ny):
        columns = slice(block * cols, (block + 1) * cols)
        gate_t[columns, :] = gate_v[:, columns].T
        up_t[columns, :] = up_v[:, columns].T
    every4.wait_recv()
    for i in range(plane - 1):
        mine = mine + rcv4[i].astype(F32)
    mixed = mine.astype(BF16)

    full[z, c] = mixed
    copies6 = []
    for i, (zz, cc) in enumerate(in_column):
        copy = remote(full.at[z, c], full.at[z, c], s6.at[i], r6.at[i], at(x, y, zz, cc))
        copy.start()
        copies6.append(copy)
    for copy in copies6:
        copy.wait_recv()

    every_row = full[...].astype(F32).reshape(rows, cols).astype(BF16)
    for dy in [dy for (dy,) in far_first(ny)] + [0]:
        yy = step(y, dy, ny)
        snd7[yy] = dot(pick_buf[yy], every_row).astype(BF16)
        for i, (dx, dyy) in enumerate(steps_xy):
            if dyy == dy:
                remote(
                    snd7.at[yy],
                    xin.at[here],
                    s7.at[i],
                    r7.at[i],
                    at(step(x, dx, nx), yy, z, c),
                ).start()
    copies7 = []
    for i, (dx, dy) in enumerate(steps_xy):
        xx, yy = step(x, dx, nx), step(y, dy, ny)
        copy = remote(snd7.at[yy], xin.at[here], s7.at[i], r7.at[i], at(xx, yy, z, c))
        copies7.append(copy)
    xin[here] = snd7[y]
    loads[14].wait()

    def one_block(block, carry):
        gate_sum, up_sum, squares = carry
        taken_rows = xin[block].astype(F32)
        columns = pl.ds(pl.multiple_of(block * cols, cols), cols)
        squares = squares + jnp.sum(taken_rows * taken_rows, axis=1, keepdims=True)
        scaled = (taken_rows * gain_ref[:, columns]).astype(BF16)
        gate_sum = gate_sum + dot(scaled, gate_t[columns, :])
        up_sum = up_sum + dot(scaled, up_t[columns, :])
        return gate_sum, up_sum, squares

    hidden_units = gate_v.shape[0]
    carry = (
        jnp.zeros((CAPACITY, hidden_units), F32),
        jnp.zeros((CAPACITY, hidden_units), F32),
        jnp.zeros((CAPACITY, 1), F32),
    )
    carry = one_block(here, carry)
    for i in range(nx * ny - 1):
        dx, dy = steps_xy[i]
        copies7[i].wait_recv()
        carry = one_block(step(x, nx - dx, nx) * ny + step(y, ny - dy, ny), carry)
    gate_sum, up_sum, squares = carry
    scale = lax.rsqrt(squares / (nx * ny * cols) + EPSILON)
    gate_sum = gate_sum * scale
    up_sum = up_sum * scale
    hidden = (gate_sum / (1.0 + jnp.exp(-gate_sum)) * up_sum).astype(BF16)

    def down_block(block):
        columns = pl.ds(pl.multiple_of(block * cols, cols), cols)
        return dot(hidden, down_v[:, columns]).astype(BF16)

    copies8 = []
    for i, (dx, dy) in enumerate(steps_xy):
        xx, yy = step(x, dx, nx), step(y, dy, ny)
        snd8[i] = down_block(xx * ny + yy)
        copy = remote(snd8.at[i], rcv8.at[here], s8.at[i], r8.at[i], at(xx, yy, z, c))
        copy.start()
        copies8.append(copy)
    rcv8[here] = down_block(here)
    for copy in copies8:
        copy.wait_recv()

    summed = []
    for yy in range(ny):
        term = rcv8[yy].astype(F32)
        for xx in range(1, nx):
            term = term + rcv8[xx * ny + yy].astype(F32)
        summed.append(term * slot_weights[yy])
    summed = jnp.concatenate(summed, axis=0).astype(BF16)
    routed = dot(pick, summed, ((0,), (0,)))
    own9[...] = routed.reshape(nz, CORES, half, cols)

    snd9[...] = own9[:, 1 - c].astype(BF16)
    copy9 = remote(snd9, rcv9, s9.at[0], r9.at[0], other)
    copy9.start()
    own9[z, c] += mixed.astype(F32)
    copy9.wait_recv()
    for zz in range(nz):
        block = own9[zz, c] + rcv9[zz].astype(F32)
        for yy in range(ny):
            snd10[yy * nz + zz] = block[2 * yy : 2 * yy + 2, :]
    for yy, zz in in_plane:
        remote(
            snd10.at[yy * nz + zz],
            rcv10.at[place_yz],
            s10.at[0],
            r10.at[0],
            at(x, yy, zz, c),
        ).start()
    rcv10[place_yz] = snd10[place_yz]
    every10 = all_of(snd10, rcv10, s10.at[0], r10.at[0])
    every10.wait_recv()
    for yy in range(ny):
        total = rcv10[yy * nz]
        for zz in range(1, nz):
            total = total + rcv10[yy * nz + zz]
        out_ref[:, yy * cols : (yy + 1) * cols] = total.astype(BF16)

    for copy in [copy_wo, every1, every4, copy9, every10]:
        copy.wait_send()
    for copy in copies2 + copies6 + copies7 + copies8:
        copy.wait_send()


def body(
    grid,
    residual_in,
    queries,
    keys_new,
    values_new,
    cached_state,
    incoming_state,
    admit_slot,
    occupancy,
    decay_rate,
    out_proj,
    norm_gain,
    routes,
    route_weight,
    gate_proj,
    up_proj,
    down_proj,
):
    nx, ny, nz = grid
    slots, hd = queries.shape
    rows = nx * slots
    half = 2 * ny
    plane = ny * nz
    cols = residual_in.shape[1] // ny
    blocks = nx * ny
    units = gate_proj.shape[2]
    width = gate_proj.shape[1]
    admitted, parts, kb, _ = incoming_state.shape

    vmem = pl.BlockSpec(memory_space=pltpu.VMEM)
    anywhere = pl.BlockSpec(memory_space=pl.ANY)
    dma = lambda n: pltpu.SemaphoreType.DMA((n,))
    scratch = [
        pltpu.VMEM((parts, admitted * kb, hd), F32),
        pltpu.SMEM(admit_slot.shape, jnp.int32),
        pltpu.VMEM((1, slots), jnp.int32),
        pltpu.VMEM((slots, hd), BF16),
        pltpu.VMEM((slots, hd), BF16),
        pltpu.VMEM((slots, hd), BF16),
        pltpu.VMEM((1, 1), F32),
        pltpu.VMEM((routes.shape[1], rows), jnp.int32),
        pltpu.VMEM((routes.shape[1], rows), F32),
        pltpu.VMEM(residual_in.shape, BF16),
        pltpu.VMEM((1, width), F32),
        pltpu.VMEM((slots * hd, hd), F32),
        pltpu.VMEM((CORES,) + out_proj.shape, BF16),
        pltpu.VMEM((units, width), BF16),
        pltpu.VMEM((units, width), BF16),
        pltpu.VMEM((units, width), BF16),
        pltpu.VMEM((width, units), BF16),
        pltpu.VMEM((width, units), BF16),
        pltpu.VMEM((parts, admitted * kb, hd), BF16),
        pltpu.VMEM((parts, admitted * kb, hd), BF16),
        pltpu.VMEM((CORES, nx, slots, hd), BF16),
        pltpu.VMEM((ny, nz, half, cols), F32),
        pltpu.VMEM((plane, half, cols), BF16),
        pltpu.VMEM((plane, half, cols), BF16),
        pltpu.VMEM((nz, CORES, half, cols), BF16),
        pltpu.VMEM((ny, CAPACITY, rows), BF16),
        pltpu.VMEM((ny, CAPACITY, cols), BF16),
        pltpu.VMEM((blocks, CAPACITY, cols), BF16),
        pltpu.VMEM((blocks, CAPACITY, cols), BF16),
        pltpu.VMEM((blocks, CAPACITY, cols), BF16),
        pltpu.VMEM((nz, CORES, half, cols), F32),
        pltpu.VMEM((nz, half, cols), BF16),
        pltpu.VMEM((nz, half, cols), BF16),
        pltpu.VMEM((plane, 2, cols), F32),
        pltpu.VMEM((plane, 2, cols), F32),
        dma(admitted + 15),
    ]
    for n in (1, nx * CORES - 1, 1, 1, nz * CORES - 1, blocks - 1, blocks - 1, 1, 1):
        scratch += [dma(n), dma(n)]

    def kernel(*refs):
        layer_kernel(grid, refs[:16], *refs[16:])

    return pl.pallas_call(
        kernel,
        out_shape=pltpu.VMEM(residual_in.shape, BF16),
        in_specs=[anywhere] * 16,
        out_specs=vmem,
        scratch_shapes=scratch,
        compiler_params=pltpu.CompilerParams(
            collective_id=0, has_side_effects=True, vmem_limit_bytes=VMEM_BYTES
        ),
    )(
        incoming_state,
        admit_slot,
        occupancy.reshape(1, slots),
        queries,
        keys_new,
        values_new,
        decay_rate.reshape(1, 1),
        cached_state.reshape(slots * hd, hd),
        routes.T,
        route_weight.T,
        residual_in,
        out_proj,
        norm_gain.reshape(1, width),
        gate_proj[0].T,
        up_proj[0].T,
        down_proj[0],
    )


def solution(mesh):
    in_specs = (
        P("ep", "sec"),
        P("sec", "ep"),
        P("sec", "ep"),
        P("sec", "ep"),
        P("sec", "ep", None, None),
        P("sec", None, "ep", None),
        P("sec"),
        P("sec"),
        P("ep"),
        P("ep", "sec"),
        P(),
        P(),
        P(),
        P("ep", None, "sec"),
        P("ep", None, "sec"),
        P("ep", "sec", None),
    )
    return jax.shard_map(
        functools.partial(body, GRID),
        mesh=mesh,
        in_specs=in_specs,
        out_specs=P("ep", "sec"),
        check_vma=False,
    )
```
